32 devices in a mesh: groups: 2 (over y), lat: 4 (over x, core), lon: 4 (over z).
Axes of the slice: x: 2, y: 2, z: 4, core: 2. Of those that a mesh axis runs over, the one named last changes fastest.
Arguments:
- fields: bfloat16 [512, 4, 512], P('groups', 'lat', 'lon'), parts along dimension 0, may hold values from -6 to 6
- upstream: bfloat16 [512, 4, 512], P('groups', 'lat', 'lon'), parts along dimension 0, may hold values from -6 to 6
- weights: bfloat16 [9, 256, 256], replicated, may hold values from -0.125 to 0.125
- filter_taps: bfloat16 [4, 9, 3, 2, 64], P('lat'), may hold values from -0.3125 to 0.3125
- cycle_counts: int32 [4], P('lat'), may hold values from 1 to 2, as said below
- cycle_blocks: int32 [4, 2], P('lat'), may hold values from -2 to 1, as said below
Outputs:
- outputs: bfloat16 [512, 4, 512], P('groups', 'lat', 'lon'), parts along dimension 0
- input_grad: bfloat16 [512, 4, 512], P('groups', 'lat', 'lon'), parts along dimension 0
- weight_grad: float32 [18, 256, 256], P('groups', 'lon'), parts along dimension 0
The draws below stay inside these ranges and needn't reach their ends.
There are 2 independent parts, one for each index of `groups`. The reference program is written for one: setup_inputs(seed, part) draws one part's arguments, and reference() takes and returns one part's arrays. A program takes and returns all parts, laid end to end along the dimension named above; an argument that names none is the same for every part. Nothing has to cross between parts.
Inputs may be any that keep to these rules, and one draw needn't show every extreme that they name: Cycle i uses its first cycle_counts[i] slots; the first quarter of the cycles (at least one) uses all 2, the last cycle one. `cycle_blocks`: the 2 block numbers of a cycle are distinct; the first cycle holds the lowest and the highest.
All inputs are finite; a program needn't handle non-finite values.
Results may differ from the reference program's by a relative error of at most 0.0049.
Values may be sent and summed in bfloat16 or wider, within the bound.
A program may use at most 64 MiB of HBM per device.

```python
import math
import jax
import jax.numpy as jnp
from jax import lax

C = 256
K = 9
BW = 64
MAXB = 2
HALO = 128
LON_DEV = 128
NLAT = 4
NLON = 512
N_LON = 4


def draw_cycle_counts(key, part):
    cycle_ids = jnp.arange(NLAT, dtype=jnp.int32)
    slot_counts = jax.random.randint(key, (NLAT,), 1, MAXB + 1, dtype=jnp.int32)
    polar_cycles = cycle_ids < max(NLAT // 4, 1)
    slot_counts = jnp.where(polar_cycles, MAXB, slot_counts)
    slot_counts = jnp.where(cycle_ids == NLAT - 1, 1, slot_counts)
    return slot_counts.astype(jnp.int32)


def draw_cycle_blocks(key, part):
    reach_blocks = HALO // BW
    cycle_keys = jax.random.split(key, NLAT)
    orders = jax.vmap(lambda cycle_key: jax.random.permutation(cycle_key, 2 * reach_blocks))(cycle_keys)
    chosen = orders[:, :MAXB].astype(jnp.int32) - reach_blocks
    first_row = jnp.where(jnp.arange(MAXB, dtype=jnp.int32) == 0, -reach_blocks, reach_blocks - 1)
    cycle_ids = jnp.arange(NLAT, dtype=jnp.int32)
    return jnp.where(cycle_ids[:, None] == 0, first_row[None, :], chosen).astype(jnp.int32)


def spiked(values, stream_key, source, target, blocks, factor):
    def block_of(axis_at):
        return (jnp.arange(values.shape[axis_at]) // (values.shape[axis_at] // blocks)).reshape((-1,) + (1,) * (values.ndim - 1 - axis_at))

    near = jax.random.permutation(stream_key, blocks)[block_of(target)]
    far = (block_of(target) + blocks // 2) % blocks
    return jnp.where((block_of(source) == near) | (block_of(source) == far), factor * values, values)


def shard_levels(key, shape, cuts, low, high):
    gain = 1.0
    for dim, parts in cuts:
        steps = jax.random.uniform(jax.random.fold_in(jax.random.fold_in(key, 6), dim), (parts,), jnp.float32, low / len(cuts), high / len(cuts))
        gain = gain * jnp.repeat(jnp.exp(steps), shape[dim] // parts).reshape((-1,) + (1,) * (len(shape) - 1 - dim))
    return gain


def noise(rng, dims, deviation, reach, shards=(), kind=jnp.bfloat16):
    factor_of = shard_levels(rng, dims, shards, -0.22, 0.18) if shards else 1.0
    drawn = jax.random.normal(rng, dims, jnp.float32) * deviation * factor_of
    return jnp.minimum(jnp.maximum(drawn, -reach), reach).astype(kind)


def noise_with(stream_key, shape, spread, reach, cuts, heavy, kind=jnp.bfloat16):
    result = spread * jax.random.normal(stream_key, shape, jnp.float32)
    if cuts:
        result = result * shard_levels(stream_key, shape, cuts, -0.22, 0.18)
    return jnp.clip(spiked(result, jax.random.fold_in(stream_key, 3), *heavy), -reach, reach).astype(kind)


def setup_inputs(seed: int = 0, part: int = 0) -> dict:
    keys = jax.random.split(jax.random.key(seed), 7)
    part_splits = jax.random.split(jax.random.fold_in(keys[6], part), 7)
    fields = noise(part_splits[0], (C, NLAT, NLON), 1.0, 6.0, ((1, 4), (2, 4)))
    upstream = noise_with(part_splits[1], (C, NLAT, NLON), 1.0, 6.0, ((1, 4), (2, 4)), (2, 0, 4, 2.0))
    weights = noise(keys[2], (K, C, C), (K * C) ** -0.5, 0.125)
    filter_taps = noise(keys[3], (NLAT, K, 3, MAXB, BW), (3 * MAXB * BW) ** -0.5, 0.3125, ((0, 4),))
    cycle_counts = draw_cycle_counts(jax.random.fold_in(keys[6], 71), part)
    cycle_blocks = draw_cycle_blocks(jax.random.fold_in(keys[6], 71), part)
    return {"fields": fields, "upstream": upstream, "weights": weights, "filter_taps": filter_taps, "cycle_counts": cycle_counts, "cycle_blocks": cycle_blocks}


def build_taps(filter_taps, cycle_counts, cycle_blocks):
    slot_total = cycle_blocks.shape[1]
    width_block = filter_taps.shape[4]
    offsets = jnp.arange(width_block, dtype=jnp.int32)
    places = HALO + width_block * cycle_blocks[:, :, None] + offsets[None, None, :]
    live_slots = jnp.arange(slot_total, dtype=jnp.int32)[None, :] < cycle_counts[:, None]
    positions = jnp.arange(2 * HALO, dtype=jnp.int32)
    onehot = jnp.where((places[:, :, :, None] == positions) & live_slots[:, :, None, None], 1.0, 0.0).astype(jnp.float32)
    return jnp.einsum("ikrst,istu->ikru", filter_taps.astype(jnp.float32), onehot)


def banded_matrix(tap_row, out_width, tap_reach):
    kernels = tap_row.shape[0]
    stencil_rows = tap_row.shape[1]
    window_len = out_width + tap_reach
    padded = jnp.concatenate([tap_row, jnp.zeros((kernels, stencil_rows, window_len + 1 - tap_reach), tap_row.dtype)], axis=2)
    repeated = jnp.tile(padded, (1, 1, out_width))[:, :, :out_width * window_len]
    repeated = repeated.reshape(kernels, stencil_rows, out_width, window_len)
    return jnp.transpose(repeated, (1, 3, 0, 2))


def reference(fields, upstream, weights, filter_taps, cycle_counts, cycle_blocks):
    tap_table = build_taps(filter_taps, cycle_counts, cycle_blocks)
    block_len = LON_DEV * math.gcd(N_LON, 4)
    window_len = block_len + 2 * HALO
    block_count = NLON // block_len
    padded = jnp.pad(fields.astype(jnp.float32), ((0, 0), (1, 1), (0, 0)))
    widened = jnp.concatenate([padded[:, :, NLON - HALO:], padded, padded[:, :, :HALO]], axis=2)

    def one_cycle(position):
        position = position.astype(jnp.int32)
        cycle_rows = lax.dynamic_slice_in_dim(widened, position, 3, axis=1)
        matrix = banded_matrix(tap_table[position], block_len, 2 * HALO).reshape(3 * window_len, K * block_len)

        def one_block(block_index):
            begin_at = (block_index * block_len).astype(jnp.int32)
            window = lax.dynamic_slice_in_dim(cycle_rows, begin_at, window_len, axis=2).reshape(C, 3 * window_len)
            return jnp.dot(window, matrix, precision=lax.Precision.HIGHEST, preferred_element_type=jnp.float32)

        pieces = lax.map(one_block, jnp.arange(block_count, dtype=jnp.int32))
        return jnp.transpose(pieces.reshape(block_count, C, K, block_len), (1, 2, 0, 3)).reshape(C, K, NLON)

    response32 = jnp.transpose(lax.map(one_cycle, jnp.arange(NLAT, dtype=jnp.int32)), (1, 0, 2, 3))
    response = response32.astype(jnp.bfloat16)
    weights32 = weights.astype(jnp.float32)
    upstream32 = upstream.astype(jnp.float32)
    response_f = response.astype(jnp.float32)
    outputs = jnp.einsum("koc,cikj->oij", weights32, response_f).astype(jnp.bfloat16)
    response_grad = jnp.einsum("koc,oij->cikj", weights32, upstream32).astype(jnp.bfloat16)
    weight_grad = jnp.einsum("oij,cikj->koc", upstream32, response_f)
    grad32 = response_grad.astype(jnp.float32)

    def per_cycle(position, accumulated):
        position = position.astype(jnp.int32)
        matrix = banded_matrix(tap_table[position], block_len, 2 * HALO).reshape(3 * window_len, K * block_len)
        grad_row = lax.dynamic_index_in_dim(grad32, position, axis=1, keepdims=False)

        def per_block(block_index, inner_acc):
            begin_at = (block_index * block_len).astype(jnp.int32)
            grad_piece = lax.dynamic_slice_in_dim(grad_row, begin_at, block_len, axis=2).reshape(C, K * block_len)
            contrib = jnp.dot(grad_piece, matrix.T, precision=lax.Precision.HIGHEST, preferred_element_type=jnp.float32)
            contrib = contrib.reshape(C, 3, window_len)
            anchor = (jnp.zeros((), jnp.int32), position, begin_at)
            current = lax.dynamic_slice(inner_acc, anchor, (C, 3, window_len))
            return lax.dynamic_update_slice(inner_acc, current + contrib, anchor)

        return lax.fori_loop(0, block_count, per_block, accumulated)

    accumulated = jnp.zeros((C, NLAT + 2, NLON + 2 * HALO), jnp.float32)
    accumulated = lax.fori_loop(0, NLAT, per_cycle, accumulated)
    interior = accumulated[:, 1:NLAT + 1, HALO:HALO + NLON]
    interior = interior.at[:, :, :HALO].add(accumulated[:, 1:NLAT + 1, NLON + HALO:])
    interior = interior.at[:, :, NLON - HALO:].add(accumulated[:, 1:NLAT + 1, :HALO])
    return outputs, interior.astype(jnp.bfloat16), weight_grad
```

```python
import functools

import jax
import jax.numpy as jnp
from jax import lax
from jax.experimental import pallas as pl
from jax.experimental.pallas import tpu as pltpu
from jax.sharding import PartitionSpec as P

HALO = 128
MESH = pl.DeviceIdType.MESH
NT = (((1,), (1,)), ((), ()))
TN = (((0,), (0,)), ((), ()))


def tap_rows(filter_taps, cycle_counts, cycle_blocks):
    kernels, stencil, slots, width = filter_taps.shape[1:]
    taps = filter_taps[0].astype(jnp.float32)
    live = jnp.arange(slots, dtype=jnp.int32) < cycle_counts[0]
    pieces = []
    for block in range(2 * HALO // width):
        here = live & (cycle_blocks[0] + HALO // width == block)
        pieces.append(jnp.sum(jnp.where(here[None, None, :, None], taps, 0.0), axis=2))
    table = jnp.concatenate(pieces, axis=2).reshape(kernels * stencil, 2 * HALO)
    return jnp.pad(table, ((0, 0), (0, 2 * HALO)))


def kernel(
    n_lat, n_lon, taps_ref, f_ref, u_ref, w_ref, out_ref, grad_ref, wg_ref,
    f_all, u_all, u_chunk, band, resp, rg, g_mine, g_got,
    part, part_got, chip, result,
    zf_s, zf_r, zu_s, zu_r, lf_s, lf_r, g_s, g_r, p_s, p_r, x_s, x_r, q_s, q_r,
):
    kernels, channels, _ = w_ref.shape
    width = f_ref.shape[1]
    chunk = u_chunk.shape[1]
    chips = n_lat // 2
    a = lax.axis_index("lat")
    b = lax.axis_index("lon")
    core = lax.rem(a, 2)
    chip_at = a // 2
    twin = a + 1 - 2 * core
    has_up = a < n_lat - 1
    has_down = a > 0

    def lon_peer(step):
        return {"lat": a, "lon": lax.rem(b + step, n_lon)}

    def lat_peer(at):
        return {"lat": at, "lon": b}

    barrier = pltpu.get_barrier_semaphore()
    for step in range(1, n_lon):
        pl.semaphore_signal(barrier, inc=1, device_id=lon_peer(step), device_id_type=MESH)
    for step in range(1, n_lat):
        pl.semaphore_signal(
            barrier, inc=1, device_id=lat_peer(lax.rem(a + step, n_lat)), device_id_type=MESH
        )
    pl.semaphore_wait(barrier, n_lon + n_lat - 2)

    def remote(src, dst, send, recv, to):
        return pltpu.make_async_remote_copy(
            src_ref=src, dst_ref=dst, send_sem=send, recv_sem=recv, device_id=to,
            device_id_type=MESH,
        )

    def send_f(step):
        slot = n_lon - step
        return remote(f_ref, f_all.at[1, slot], zf_s.at[step], zf_r.at[slot], lon_peer(step))

    def send_u(step):
        slot = n_lon - step
        if step in (1, n_lon - 1):
            return remote(u_ref, u_all.at[slot], zu_s.at[step], zu_r.at[slot], lon_peer(step))
        start = pl.multiple_of(lax.rem(b + step, n_lon) * chunk, chunk)
        return remote(
            u_ref.at[pl.ds(start, chunk)], u_chunk.at[slot], zu_s.at[step], zu_r.at[slot],
            lon_peer(step),
        )

    def lat_f(way, slot):
        to = a + 1 if way == 0 else a - 1
        src = f_ref if slot == 0 else f_all.at[1, slot]
        return remote(
            src, f_all.at[2 * way, slot], lf_s.at[way, slot], lf_r.at[way, slot], lat_peer(to)
        )

    steps = sorted(range(1, n_lon), key=lambda step: min(step, n_lon - step), reverse=True)
    for step in steps:
        send_f(step).start()

    @pl.when(has_up)
    def _():
        lat_f(0, 0).start()

    @pl.when(has_down)
    def _():
        lat_f(1, 0).start()

    for step in steps:
        send_u(step).start()

    for k in range(kernels):
        for r in range(3):
            row = taps_ref[3 * k + r : 3 * k + r + 1, :]
            turned = pltpu.roll(
                jnp.broadcast_to(row, (width, 4 * HALO)), 0, 1, stride=1, stride_axis=0
            ).astype(jnp.bfloat16)
            for d in range(3):
                band[k * width : (k + 1) * width, (3 * d + r) * width : (3 * d + r + 1) * width] = (
                    turned[:, d * width : (d + 1) * width]
                )

    f_all[1, 0] = f_ref[...]
    u_all[0] = u_ref[...]

    @pl.when(jnp.logical_not(has_down))
    def _():
        f_all[0] = jnp.zeros(f_all.shape[1:], f_all.dtype)

    @pl.when(jnp.logical_not(has_up))
    def _():
        f_all[2] = jnp.zeros(f_all.shape[1:], f_all.dtype)

    for step in steps[::-1]:
        slot = n_lon - step
        send_f(step).wait_recv()

        @pl.when(has_up)
        def _():
            lat_f(0, slot).start()

        @pl.when(has_down)
        def _():
            lat_f(1, slot).start()

    for step in (1, n_lon - 1):
        send_u(step).wait_recv()
    u_wide = jnp.concatenate([u_all[n_lon - 1], u_all[0], u_all[1]], axis=1)
    for k in range(kernels):
        mixed = lax.dot_general(
            w_ref[k], u_wide, TN, preferred_element_type=jnp.float32
        ).astype(jnp.bfloat16)
        for j in range(3):
            rg[j, :, k * width : (k + 1) * width] = mixed[:, j * width : (j + 1) * width]
    terms = jnp.zeros((channels, 3 * width), jnp.float32)
    for j in range(3):
        terms = terms + jnp.dot(
            rg[j], band[:, (2 - j) * 3 * width : (3 - j) * 3 * width],
            preferred_element_type=jnp.float32,
        )
    for r in range(3):
        g_mine[r] = terms[:, r * width : (r + 1) * width]

    def send_g(way):
        to = a + 1 if way == 0 else a - 1
        return remote(g_mine.at[2 - 2 * way], g_got.at[way], g_s.at[way], g_r.at[way], lat_peer(to))

    @pl.when(has_up)
    def _():
        send_g(0).start()

    @pl.when(has_down)
    def _():
        send_g(1).start()

    for slot in range(n_lon):
        @pl.when(has_down)
        def _():
            lat_f(0, slot).wait_recv()

        @pl.when(has_up)
        def _():
            lat_f(1, slot).wait_recv()

    group = 3 if kernels % 3 == 0 else 1

    @pl.loop(0, n_lon)
    def _(slot):
        window = jnp.concatenate(
            [f_all[r, lax.rem(slot + n_lon - 1 + d, n_lon)] for d in range(3) for r in range(3)],
            axis=1,
        )
        for k0 in range(0, kernels, group):
            got = lax.dot_general(
                window, band[k0 * width : (k0 + group) * width, :], NT,
                preferred_element_type=jnp.float32,
            ).astype(jnp.bfloat16)
            for k in range(group):
                resp[k0 + k, slot] = got[:, k * width : (k + 1) * width]

    rows = pl.ds(pl.multiple_of(b * chunk, chunk), chunk)
    for step in range(2, n_lon - 1):
        send_u(step).wait_recv()
    for slot in (0, 1, n_lon - 1):
        u_chunk[slot] = u_all[slot, rows, :]
    u_line = jnp.concatenate([u_chunk[slot] for slot in range(n_lon)], axis=1)
    for k in range(kernels):
        line = jnp.concatenate([resp[k, slot] for slot in range(n_lon)], axis=1)
        piece = lax.dot_general(u_line, line, NT, preferred_element_type=jnp.float32)
        for half in range(2):
            part[half, k * chunk : (k + 1) * chunk, :] = piece[
                :, half * channels // 2 : (half + 1) * channels // 2
            ]

    send_p = remote(part.at[1 - core], part_got, p_s, p_r, lat_peer(twin))
    send_p.start()

    def mix_out():
        total = jnp.zeros((channels, width), jnp.float32)
        for k in range(kernels):
            total = total + jnp.dot(w_ref[k], resp[k, 0], preferred_element_type=jnp.float32)
        out_ref[...] = total.astype(out_ref.dtype)

    send_p.wait_recv()
    chip[chip_at] = (part[core] + part_got[...]).astype(chip.dtype)

    def send_x(step):
        to = lax.rem(a + 2 * step, n_lat)
        return remote(
            chip.at[chip_at], chip.at[chip_at], x_s.at[step], x_r.at[chips - step], lat_peer(to)
        )

    def got_x(step):
        at = lax.rem(chip_at + chips - step, chips)
        return remote(
            chip.at[at], chip.at[at], x_s.at[step], x_r.at[chips - step], lat_peer(twin)
        )

    for step in range(1, chips):
        send_x(step).start()

    mix_out()

    @pl.when(has_down)
    def _():
        send_g(0).wait_recv()

    @pl.when(has_up)
    def _():
        send_g(1).wait_recv()

    below = jnp.where(has_down, g_got[0], 0.0)
    above = jnp.where(has_up, g_got[1], 0.0)
    grad_ref[...] = (g_mine[1] + below + above).astype(grad_ref.dtype)

    for step in range(1, chips):
        got_x(step).wait_recv()
    total = chip[0].astype(jnp.float32)
    for at in range(1, chips):
        total = total + chip[at].astype(jnp.float32)
    result[core] = total
    send_q = remote(result.at[core], result.at[core], q_s, q_r, lat_peer(twin))
    send_q.start()
    remote(result.at[1 - core], result.at[1 - core], q_s, q_r, lat_peer(twin)).wait_recv()
    wg_ref[:, : channels // 2] = result[0]
    wg_ref[:, channels // 2 :] = result[1]

    for step in range(1, n_lon):
        send_f(step).wait_send()
        send_u(step).wait_send()
    for slot in range(n_lon):
        @pl.when(has_up)
        def _():
            lat_f(0, slot).wait_send()

        @pl.when(has_down)
        def _():
            lat_f(1, slot).wait_send()

    @pl.when(has_up)
    def _():
        send_g(0).wait_send()

    @pl.when(has_down)
    def _():
        send_g(1).wait_send()

    send_p.wait_send()
    for step in range(1, chips):
        send_x(step).wait_send()
    send_q.wait_send()


def body(fields, upstream, weights, filter_taps, cycle_counts, cycle_blocks):
    channels, _, width = fields.shape
    kernels = weights.shape[0]
    n_lat, n_lon = lax.axis_size("lat"), lax.axis_size("lon")
    chunk = channels // n_lon
    taps = tap_rows(filter_taps, cycle_counts, cycle_blocks)
    bf16, f32 = jnp.bfloat16, jnp.float32
    dma = pltpu.SemaphoreType.DMA
    outputs, grad, weight_grad = pl.pallas_call(
        functools.partial(kernel, n_lat, n_lon),
        out_shape=(
            jax.ShapeDtypeStruct((channels, width), bf16),
            jax.ShapeDtypeStruct((channels, width), bf16),
            jax.ShapeDtypeStruct((kernels * chunk, channels), f32),
        ),
        in_specs=[pl.BlockSpec(memory_space=pltpu.VMEM)] * 4,
        out_specs=[pl.BlockSpec(memory_space=pltpu.VMEM)] * 3,
        scratch_shapes=[
            pltpu.VMEM((3, n_lon, channels, width), bf16),
            pltpu.VMEM((n_lon, channels, width), bf16),
            pltpu.VMEM((n_lon, chunk, width), bf16),
            pltpu.VMEM((kernels * width, 9 * width), bf16),
            pltpu.VMEM((kernels, n_lon, channels, width), bf16),
            pltpu.VMEM((3, channels, kernels * width), bf16),
            pltpu.VMEM((3, channels, width), f32),
            pltpu.VMEM((2, channels, width), f32),
            pltpu.VMEM((2, kernels * chunk, channels // 2), f32),
            pltpu.VMEM((kernels * chunk, channels // 2), f32),
            pltpu.VMEM((n_lat // 2, kernels * chunk, channels // 2), bf16),
            pltpu.VMEM((2, kernels * chunk, channels // 2), f32),
            dma((n_lon,)), dma((n_lon,)), dma((n_lon,)), dma((n_lon,)),
            dma((2, n_lon)), dma((2, n_lon)), dma((2,)), dma((2,)),
            dma, dma, dma((n_lat // 2,)), dma((n_lat // 2 + 1,)), dma, dma,
        ],
        compiler_params=pltpu.CompilerParams(
            collective_id=0, has_side_effects=True, vmem_limit_bytes=56 * 1024 * 1024
        ),
        cost_estimate=pl.CostEstimate(
            flops=8_000_000_000, bytes_accessed=3_000_000, transcendentals=0
        ),
    )(taps, fields.reshape(channels, width), upstream.reshape(channels, width), weights)
    return (
        outputs.reshape(fields.shape),
        grad.reshape(fields.shape),
        weight_grad.reshape(kernels, chunk, channels),
    )


def solution(mesh):
    return jax.shard_map(
        body,
        mesh=mesh,
        in_specs=(
            P("groups", "lat", "lon"),
            P("groups", "lat", "lon"),
            P(),
            P("lat", None, None, None, None),
            P("lat"),
            P("lat", None),
        ),
        out_specs=(P("groups", "lat", "lon"), P("groups", "lat", "lon"), P("groups", "lon", None)),
        check_vma=False,
    )
```

```python
import functools

import jax
import jax.numpy as jnp
from jax import lax
from jax.experimental import pallas as pl
from jax.experimental.pallas import tpu as pltpu
from jax.sharding import PartitionSpec as P

HALO = 128
MESH = pl.DeviceIdType.MESH
NT = (((1,), (1,)), ((), ()))
TN = (((0,), (0,)), ((), ()))


def finish(*refs):
    count = (len(refs) - 1) // 2
    sems = refs[-1]
    copies = [
        pltpu.make_async_copy(refs[i], refs[count + i], sems.at[i]) for i in range(count)
    ]
    for copy in copies:
        copy.start()
    for copy in copies:
        copy.wait()


def kernel(
    n_lat, n_lon, taps_ref, counts_ref, blocks_ref, f_ref, u_ref, w_ref, out_ref, grad_ref, wg_ref,
    f_all, u_all, u_chunk, band, resp, rg, g_mine, g_got,
    part, part_got, chip, result,
    zf_s, zf_r, zc_s, zc_r, zu_s, zu_r, lf_s, lf_r, g_s, g_r, p_s, p_r, x_s, x_r, q_s, q_r,
):
    kernels, channels, _ = w_ref.shape
    width = f_ref.shape[1]
    chunk = u_chunk.shape[1]
    chips = n_lat // 2
    a = lax.axis_index("lat")
    b = lax.axis_index("lon")
    core = lax.rem(a, 2)
    chip_at = a // 2
    twin = a + 1 - 2 * core
    has_up = a < n_lat - 1
    has_down = a > 0

    def lon_peer(step):
        return {"lat": a, "lon": lax.rem(b + step, n_lon)}

    def lat_peer(at):
        return {"lat": at, "lon": b}

    barrier = pltpu.get_barrier_semaphore()
    for step in range(1, n_lon):
        pl.semaphore_signal(barrier, inc=1, device_id=lon_peer(step), device_id_type=MESH)
    for step in range(1, n_lat):
        pl.semaphore_signal(
            barrier, inc=1, device_id=lat_peer(lax.rem(a + step, n_lat)), device_id_type=MESH
        )
    pl.semaphore_wait(barrier, n_lon + n_lat - 2)

    def remote(src, dst, send, recv, to):
        return pltpu.make_async_remote_copy(
            src_ref=src, dst_ref=dst, send_sem=send, recv_sem=recv, device_id=to,
            device_id_type=MESH,
        )

    def send_f(step):
        slot = n_lon - step
        return remote(f_ref, f_all.at[1, slot], zf_s.at[step], zf_r.at[slot], lon_peer(step))

    def send_chunk(step):
        slot = n_lon - step
        start = pl.multiple_of(lax.rem(b + step, n_lon) * chunk, chunk)
        return remote(
            u_ref.at[pl.ds(start, chunk)], u_chunk.at[slot], zc_s.at[step], zc_r.at[slot],
            lon_peer(step),
        )

    def send_u(step):
        slot = n_lon - step
        return remote(u_ref, u_all.at[slot], zu_s.at[step], zu_r.at[slot], lon_peer(step))

    def lat_f(way, slot):
        to = a + 1 if way == 0 else a - 1
        src = f_ref if slot == 0 else f_all.at[1, slot]
        return remote(
            src, f_all.at[2 * way, slot], lf_s.at[way, slot], lf_r.at[way, slot], lat_peer(to)
        )

    steps = sorted(range(1, n_lon), key=lambda step: min(step, n_lon - step), reverse=True)
    for step in steps:
        send_f(step).start()

    @pl.when(has_up)
    def _():
        lat_f(0, 0).start()

    @pl.when(has_down)
    def _():
        lat_f(1, 0).start()

    for step in steps:
        send_chunk(step).start()
    for step in (1, n_lon - 1):
        send_u(step).start()

    slots, block_width = taps_ref.shape[3:]
    lane = lax.broadcasted_iota(jnp.int32, (slots, 4 * HALO), 1)
    which = lax.broadcasted_iota(jnp.int32, (slots, 4 * HALO), 0)
    first = jnp.zeros((slots, 4 * HALO), jnp.int32)
    for s in range(slots):
        first = jnp.where(which == s, HALO + block_width * blocks_ref[0, s], first)
    used = (which < counts_ref[0]) & (lane >= first) & (lane < first + block_width)
    rest = jnp.zeros((slots, 2 * HALO), jnp.float32)
    for k in range(kernels):
        for r in range(3):
            tile = taps_ref[0, k, r].astype(jnp.float32)
            spread = jnp.concatenate([tile] * (2 * HALO // block_width) + [rest], axis=1)
            row = jnp.sum(jnp.where(used, spread, 0.0), axis=0, keepdims=True)
            turned = pltpu.roll(
                jnp.broadcast_to(row, (width, 4 * HALO)), 0, 1, stride=1, stride_axis=0
            ).astype(jnp.bfloat16)
            for d in range(3):
                band[k * width : (k + 1) * width, (3 * d + r) * width : (3 * d + r + 1) * width] = (
                    turned[:, d * width : (d + 1) * width]
                )

    f_all[1, 0] = f_ref[...]

    @pl.when(jnp.logical_not(has_down))
    def _():
        f_all[0] = jnp.zeros(f_all.shape[1:], f_all.dtype)

    @pl.when(jnp.logical_not(has_up))
    def _():
        f_all[2] = jnp.zeros(f_all.shape[1:], f_all.dtype)

    for step in steps[::-1]:
        slot = n_lon - step
        send_f(step).wait_recv()

        @pl.when(has_up)
        def _():
            lat_f(0, slot).start()

        @pl.when(has_down)
        def _():
            lat_f(1, slot).start()

    def wait_lat(slot):
        @pl.when(has_down)
        def _():
            lat_f(0, slot).wait_recv()

        @pl.when(has_up)
        def _():
            lat_f(1, slot).wait_recv()

    group = 3 if kernels % 3 == 0 else 1
    groups = kernels // group

    def convolve(slot):
        window = jnp.concatenate(
            [f_all[r, lax.rem(slot + n_lon - 1 + d, n_lon)] for d in range(3) for r in range(3)],
            axis=1,
        )
        for k0 in range(0, kernels, group):
            got = lax.dot_general(
                window, band[k0 * width : (k0 + group) * width, :], NT,
                preferred_element_type=jnp.float32,
            ).astype(jnp.bfloat16)
            for k in range(group):
                resp[k0 + k, slot] = got[:, k * width : (k + 1) * width]

    for slot in (0, 1, n_lon - 1):
        wait_lat(slot)
    convolve(0)
    for slot in range(2, n_lon - 1):
        wait_lat(slot)
    pl.loop(1, n_lon)(convolve)

    u_chunk[0] = u_ref[pl.ds(pl.multiple_of(b * chunk, chunk), chunk), :]
    for step in range(1, n_lon):
        send_chunk(step).wait_recv()
    u_line = jnp.concatenate([u_chunk[slot] for slot in range(n_lon)], axis=1)

    def send_p(g):
        return remote(
            part.at[1 - core, g], part_got.at[g], p_s.at[g], p_r.at[g], lat_peer(twin)
        )

    for g in range(groups):
        for k in range(group):
            line = jnp.concatenate(
                [resp[g * group + k, slot] for slot in range(n_lon)], axis=1
            )
            piece = lax.dot_general(u_line, line, NT, preferred_element_type=jnp.float32)
            for half in range(2):
                part[half, g, k * chunk : (k + 1) * chunk, :] = piece[
                    :, half * channels // 2 : (half + 1) * channels // 2
                ]
        send_p(g).start()

    def send_x(g, step):
        to = lax.rem(a + 2 * step, n_lat)
        return remote(
            chip.at[chip_at, g], chip.at[chip_at, g], x_s.at[g, step],
            x_r.at[g, chips - step], lat_peer(to),
        )

    def got_x(g, step):
        at = lax.rem(chip_at + chips - step, chips)
        return remote(
            chip.at[at, g], chip.at[at, g], x_s.at[g, step], x_r.at[g, chips - step],
            lat_peer(twin),
        )

    for g in range(groups):
        send_p(g).wait_recv()
        chip[chip_at, g] = (part[core, g] + part_got[g]).astype(chip.dtype)
        for step in range(1, chips):
            send_x(g, step).start()

    u_all[0] = u_ref[...]
    for step in (1, n_lon - 1):
        send_u(step).wait_recv()
    u_wide = jnp.concatenate([u_all[n_lon - 1], u_all[0], u_all[1]], axis=1)
    for k in range(kernels):
        mixed = lax.dot_general(
            w_ref[k], u_wide, TN, preferred_element_type=jnp.float32
        ).astype(jnp.bfloat16)
        for j in range(3):
            rg[j, :, k * width : (k + 1) * width] = mixed[:, j * width : (j + 1) * width]
    terms = jnp.zeros((channels, 3 * width), jnp.float32)
    for j in range(3):
        terms = terms + jnp.dot(
            rg[j], band[:, (2 - j) * 3 * width : (3 - j) * 3 * width],
            preferred_element_type=jnp.float32,
        )
    for r in range(3):
        g_mine[r] = terms[:, r * width : (r + 1) * width]

    def send_g(way):
        to = a + 1 if way == 0 else a - 1
        return remote(g_mine.at[2 - 2 * way], g_got.at[way], g_s.at[way], g_r.at[way], lat_peer(to))

    @pl.when(has_up)
    def _():
        send_g(0).start()

    @pl.when(has_down)
    def _():
        send_g(1).start()

    mixed = jnp.zeros((channels, width), jnp.float32)
    for k in range(kernels):
        mixed = mixed + jnp.dot(w_ref[k], resp[k, 0], preferred_element_type=jnp.float32)
    out_ref[...] = mixed.astype(out_ref.dtype)

    def send_q(g):
        return remote(result.at[core, g], result.at[core, g], q_s.at[g], q_r.at[g], lat_peer(twin))

    def got_q(g):
        return remote(
            result.at[1 - core, g], result.at[1 - core, g], q_s.at[g], q_r.at[g], lat_peer(twin)
        )

    for g in range(groups):
        for step in range(1, chips):
            got_x(g, step).wait_recv()
        total = chip[0, g].astype(jnp.float32)
        for at in range(1, chips):
            total = total + chip[at, g].astype(jnp.float32)
        result[core, g] = total
        send_q(g).start()

    @pl.when(has_down)
    def _():
        send_g(0).wait_recv()

    @pl.when(has_up)
    def _():
        send_g(1).wait_recv()

    below = jnp.where(has_down, g_got[0], 0.0)
    above = jnp.where(has_up, g_got[1], 0.0)
    grad_ref[...] = (g_mine[1] + below + above).astype(grad_ref.dtype)

    for g in range(groups):
        got_q(g).wait_recv()
        rows = slice(g * group * chunk, (g + 1) * group * chunk)
        wg_ref[rows, : channels // 2] = result[0, g]
        wg_ref[rows, channels // 2 :] = result[1, g]

    for step in range(1, n_lon):
        send_f(step).wait_send()
        send_chunk(step).wait_send()
    for step in (1, n_lon - 1):
        send_u(step).wait_send()
    for slot in range(n_lon):
        @pl.when(has_up)
        def _():
            lat_f(0, slot).wait_send()

        @pl.when(has_down)
        def _():
            lat_f(1, slot).wait_send()

    @pl.when(has_up)
    def _():
        send_g(0).wait_send()

    @pl.when(has_down)
    def _():
        send_g(1).wait_send()

    for g in range(groups):
        send_p(g).wait_send()
        for step in range(1, chips):
            send_x(g, step).wait_send()
        send_q(g).wait_send()


def body(fields, upstream, weights, filter_taps, cycle_counts, cycle_blocks):
    channels, _, width = fields.shape
    kernels = weights.shape[0]
    n_lat, n_lon = lax.axis_size("lat"), lax.axis_size("lon")
    chunk = channels // n_lon
    groups = kernels // 3 if kernels % 3 == 0 else kernels
    rows, half = kernels // groups * chunk, channels // 2
    bf16, f32 = jnp.bfloat16, jnp.float32
    dma = pltpu.SemaphoreType.DMA
    vmem = pl.BlockSpec(memory_space=pltpu.VMEM)
    smem = pl.BlockSpec(memory_space=pltpu.SMEM)
    anywhere = pl.BlockSpec(memory_space=pl.ANY)
    results = pl.pallas_call(
        functools.partial(kernel, n_lat, n_lon),
        out_shape=(
            jax.ShapeDtypeStruct((channels, width), bf16),
            jax.ShapeDtypeStruct((channels, width), bf16),
            jax.ShapeDtypeStruct((kernels * chunk, channels), f32),
        ),
        in_specs=[vmem, smem, smem, vmem, vmem, vmem],
        out_specs=[vmem] * 3,
        scratch_shapes=[
            pltpu.VMEM((3, n_lon, channels, width), bf16),
            pltpu.VMEM((n_lon, channels, width), bf16),
            pltpu.VMEM((n_lon, chunk, width), bf16),
            pltpu.VMEM((kernels * width, 9 * width), bf16),
            pltpu.VMEM((kernels, n_lon, channels, width), bf16),
            pltpu.VMEM((3, channels, kernels * width), bf16),
            pltpu.VMEM((3, channels, width), f32),
            pltpu.VMEM((2, channels, width), f32),
            pltpu.VMEM((2, groups, rows, half), f32),
            pltpu.VMEM((groups, rows, half), f32),
            pltpu.VMEM((n_lat // 2, groups, rows, half), bf16),
            pltpu.VMEM((2, groups, rows, half), f32),
            dma((n_lon,)), dma((n_lon,)), dma((n_lon,)), dma((n_lon,)), dma((n_lon,)), dma((n_lon,)),
            dma((2, n_lon)), dma((2, n_lon)), dma((2,)), dma((2,)),
            dma((groups,)), dma((groups,)), dma((groups, n_lat // 2)), dma((groups, n_lat // 2 + 1)),
            dma((groups,)), dma((groups,)),
        ],
        compiler_params=pltpu.CompilerParams(
            collective_id=0, has_side_effects=True, vmem_limit_bytes=56 * 1024 * 1024
        ),
        cost_estimate=pl.CostEstimate(
            flops=8_000_000_000, bytes_accessed=3_000_000, transcendentals=0
        ),
    )(
        filter_taps, cycle_counts, cycle_blocks,
        fields.reshape(channels, width), upstream.reshape(channels, width), weights,
    )
    outputs, grad, weight_grad = pl.pallas_call(
        finish,
        out_shape=tuple(jax.ShapeDtypeStruct(held.shape, held.dtype) for held in results),
        in_specs=[anywhere] * 3,
        out_specs=[anywhere] * 3,
        scratch_shapes=[dma((3,))],
        compiler_params=pltpu.CompilerParams(vmem_limit_bytes=56 * 1024 * 1024),
    )(*results)
    return (
        outputs.reshape(fields.shape),
        grad.reshape(fields.shape),
        weight_grad.reshape(kernels, chunk, channels),
    )


def solution(mesh):
    return jax.shard_map(
        body,
        mesh=mesh,
        in_specs=(
            P("groups", "lat", "lon"),
            P("groups", "lat", "lon"),
            P(),
            P("lat", None, None, None, None),
            P("lat"),
            P("lat", None),
        ),
        out_specs=(P("groups", "lat", "lon"), P("groups", "lat", "lon"), P("groups", "lon", None)),
        check_vma=False,
    )
```

```python
import functools

import jax
import jax.numpy as jnp
from jax import lax
from jax.experimental import pallas as pl
from jax.experimental.pallas import tpu as pltpu
from jax.sharding import PartitionSpec as P

HALO = 128
MESH = pl.DeviceIdType.MESH


def finish(*refs):
    count = len(refs) // 2
    for i in range(count):
        refs[count + i][...] = refs[i][...]


def kernel(
    n_lat, n_lon, taps_ref, counts_ref, blocks_ref, f_ref, u_ref, w_hbm, out_ref, grad_ref, wg_ref,
    w_ref, w_turned, f_mine, f_all, u_all, u_chunk, band, resp, rg, g_mine, g_got,
    part, part_got, chip, result,
    zf_s, zf_r, zc_s, zc_r, zu_s, zu_r, lf_s, lf_r, g_s, g_r, p_s, p_r, x_s, x_r, q_s, q_r, w_s,
):
    kernels, channels, _ = w_ref.shape
    width = f_ref.shape[1]
    chunk = u_chunk.shape[1]
    chips = n_lat // 2
    a = lax.axis_index("lat")
    b = lax.axis_index("lon")
    core = lax.rem(a, 2)
    chip_at = a // 2
    twin = a + 1 - 2 * core
    has_up = a < n_lat - 1
    has_down = a > 0

    def lon_peer(step):
        return {"lat": a, "lon": lax.rem(b + step, n_lon)}

    def lat_peer(at):
        return {"lat": at, "lon": b}

    load_w = pltpu.make_async_copy(w_hbm, w_ref, w_s)
    load_w.start()
    barrier = pltpu.get_barrier_semaphore()
    for step in range(1, n_lon):
        pl.semaphore_signal(barrier, inc=1, device_id=lon_peer(step), device_id_type=MESH)
    for step in range(1, n_lat):
        pl.semaphore_signal(
            barrier, inc=1, device_id=lat_peer(lax.rem(a + step, n_lat)), device_id_type=MESH
        )
    f_mine[...] = f_ref[...].T
    pl.semaphore_wait(barrier, n_lon + n_lat - 2)

    def remote(src, dst, send, recv, to):
        return pltpu.make_async_remote_copy(
            src_ref=src, dst_ref=dst, send_sem=send, recv_sem=recv, device_id=to,
            device_id_type=MESH,
        )

    def send_f(step):
        slot = n_lon - step
        return remote(f_mine, f_all.at[slot, 1], zf_s.at[step], zf_r.at[slot], lon_peer(step))

    def send_chunk(step):
        slot = n_lon - step
        start = pl.multiple_of(lax.rem(b + step, n_lon) * chunk, chunk)
        return remote(
            u_ref.at[pl.ds(start, chunk)], u_chunk.at[slot], zc_s.at[step], zc_r.at[slot],
            lon_peer(step),
        )

    def send_u(step):
        slot = n_lon - step
        return remote(u_ref, u_all.at[slot], zu_s.at[step], zu_r.at[slot], lon_peer(step))

    def lat_f(way, slot):
        to = a + 1 if way == 0 else a - 1
        src = f_mine if slot == 0 else f_all.at[slot, 1]
        return remote(
            src, f_all.at[slot, 2 * way], lf_s.at[way, slot], lf_r.at[way, slot], lat_peer(to)
        )

    steps = sorted(range(1, n_lon), key=lambda step: min(step, n_lon - step), reverse=True)
    for step in steps:
        send_f(step).start()

    @pl.when(has_up)
    def _():
        lat_f(0, 0).start()

    @pl.when(has_down)
    def _():
        lat_f(1, 0).start()

    for step in steps:
        send_chunk(step).start()

    slots, block_width = taps_ref.shape[3:]
    lane = lax.broadcasted_iota(jnp.int32, (slots, 4 * HALO), 1)
    which = lax.broadcasted_iota(jnp.int32, (slots, 4 * HALO), 0)
    first = jnp.zeros((slots, 4 * HALO), jnp.int32)
    for s in range(slots):
        first = jnp.where(which == s, HALO + block_width * blocks_ref[0, s], first)
    used = (which < counts_ref[0]) & (lane >= first) & (lane < first + block_width)
    rest = jnp.zeros((slots, 2 * HALO), jnp.float32)
    for k in range(kernels):
        for r in range(3):
            tile = taps_ref[0, k, r].astype(jnp.float32)
            spread = jnp.concatenate([tile] * (2 * HALO // block_width) + [rest], axis=1)
            row = jnp.sum(jnp.where(used, spread, 0.0), axis=0, keepdims=True)
            turned = pltpu.roll(
                jnp.broadcast_to(row, (width, 4 * HALO)), 0, 1, stride=1, stride_axis=0
            ).astype(jnp.bfloat16)
            for d in range(3):
                band[k * width : (k + 1) * width, (3 * d + r) * width : (3 * d + r + 1) * width] = (
                    turned[:, d * width : (d + 1) * width]
                )

    load_w.wait()
    for k in range(kernels):
        w_turned[k * channels : (k + 1) * channels, :] = w_ref[k].T

    f_all[0, 1] = f_mine[...]

    @pl.when(jnp.logical_not(has_down))
    def _():
        f_all[:, 0] = jnp.zeros((n_lon, width, channels), f_all.dtype)

    @pl.when(jnp.logical_not(has_up))
    def _():
        f_all[:, 2] = jnp.zeros((n_lon, width, channels), f_all.dtype)

    for step in steps[::-1]:
        slot = n_lon - step
        send_f(step).wait_recv()

        @pl.when(has_up)
        def _():
            lat_f(0, slot).start()

        @pl.when(has_down)
        def _():
            lat_f(1, slot).start()

    for step in (1, n_lon - 1):
        send_u(step).start()

    def wait_lat(slot):
        @pl.when(has_down)
        def _():
            lat_f(0, slot).wait_recv()

        @pl.when(has_up)
        def _():
            lat_f(1, slot).wait_recv()

    group = 3 if kernels % 3 == 0 else 1
    groups = kernels // group

    def convolve(slot):
        window = jnp.concatenate(
            [f_all[lax.rem(slot + n_lon - 1 + d, n_lon), r] for d in range(3) for r in range(3)],
            axis=0,
        )
        for k0 in range(0, kernels, group):
            got = jnp.dot(
                band[k0 * width : (k0 + group) * width, :], window,
                preferred_element_type=jnp.float32,
            ).astype(jnp.bfloat16)
            for k in range(group):
                resp[k0 + k, slot] = got[k * width : (k + 1) * width]

    for slot in (0, 1, n_lon - 1):
        wait_lat(slot)
    convolve(0)
    for slot in range(2, n_lon - 1):
        wait_lat(slot)
    pl.loop(1, n_lon)(convolve)

    u_chunk[0] = u_ref[pl.ds(pl.multiple_of(b * chunk, chunk), chunk), :]
    for step in range(1, n_lon):
        send_chunk(step).wait_recv()
    u_line = jnp.concatenate([u_chunk[slot] for slot in range(n_lon)], axis=1)

    def send_p(g):
        return remote(
            part.at[1 - core, g], part_got.at[g], p_s.at[g], p_r.at[g], lat_peer(twin)
        )

    for g in range(groups):
        for k in range(group):
            line = resp[g * group + k].reshape(n_lon * width, channels)
            piece = jnp.dot(u_line, line, preferred_element_type=jnp.float32)
            for half in range(2):
                part[half, g, k * chunk : (k + 1) * chunk, :] = piece[
                    :, half * channels // 2 : (half + 1) * channels // 2
                ]
        send_p(g).start()

    def send_x(g, step):
        to = lax.rem(a + 2 * step, n_lat)
        return remote(
            chip.at[chip_at, g], chip.at[chip_at, g], x_s.at[g, step],
            x_r.at[g, chips - step], lat_peer(to),
        )

    def got_x(g, step):
        at = lax.rem(chip_at + chips - step, chips)
        return remote(
            chip.at[at, g], chip.at[at, g], x_s.at[g, step], x_r.at[g, chips - step],
            lat_peer(twin),
        )

    for g in range(groups):
        send_p(g).wait_recv()
        chip[chip_at, g] = (part[core, g] + part_got[g]).astype(chip.dtype)
        for step in range(1, chips):
            send_x(g, step).start()

    u_all[0] = u_ref[...]
    for step in (1, n_lon - 1):
        send_u(step).wait_recv()
    u_wide = jnp.concatenate([u_all[n_lon - 1], u_all[0], u_all[1]], axis=1)
    for k in range(kernels):
        mixed = jnp.dot(
            w_turned[k * channels : (k + 1) * channels, :], u_wide,
            preferred_element_type=jnp.float32,
        ).astype(jnp.bfloat16)
        for j in range(3):
            rg[j, :, k * width : (k + 1) * width] = mixed[:, j * width : (j + 1) * width]
    terms = jnp.zeros((channels, 3 * width), jnp.float32)
    for j in range(3):
        terms = terms + jnp.dot(
            rg[j], band[:, (2 - j) * 3 * width : (3 - j) * 3 * width],
            preferred_element_type=jnp.float32,
        )
    for r in range(3):
        g_mine[r] = terms[:, r * width : (r + 1) * width]

    def send_g(way):
        to = a + 1 if way == 0 else a - 1
        return remote(g_mine.at[2 - 2 * way], g_got.at[way], g_s.at[way], g_r.at[way], lat_peer(to))

    @pl.when(has_up)
    def _():
        send_g(0).start()

    @pl.when(has_down)
    def _():
        send_g(1).start()

    here = jnp.concatenate([resp[k, 0] for k in range(kernels)], axis=1)
    mixed = jnp.dot(here, w_turned[...], preferred_element_type=jnp.float32)
    out_ref[...] = mixed.astype(out_ref.dtype).T

    def send_q(g):
        return remote(result.at[core, g], result.at[core, g], q_s.at[g], q_r.at[g], lat_peer(twin))

    def got_q(g):
        return remote(
            result.at[1 - core, g], result.at[1 - core, g], q_s.at[g], q_r.at[g], lat_peer(twin)
        )

    for g in range(groups):
        for step in range(1, chips):
            got_x(g, step).wait_recv()
        total = chip[0, g].astype(jnp.float32)
        for at in range(1, chips):
            total = total + chip[at, g].astype(jnp.float32)
        result[core, g] = total
        send_q(g).start()

    @pl.when(has_down)
    def _():
        send_g(0).wait_recv()

    @pl.when(has_up)
    def _():
        send_g(1).wait_recv()

    below = jnp.where(has_down, g_got[0], 0.0)
    above = jnp.where(has_up, g_got[1], 0.0)
    grad_ref[...] = (g_mine[1] + below + above).astype(grad_ref.dtype)

    for g in range(groups):
        got_q(g).wait_recv()
        rows = slice(g * group * chunk, (g + 1) * group * chunk)
        wg_ref[rows, : channels // 2] = result[0, g]
        wg_ref[rows, channels // 2 :] = result[1, g]

    for step in range(1, n_lon):
        send_f(step).wait_send()
        send_chunk(step).wait_send()
    for step in (1, n_lon - 1):
        send_u(step).wait_send()
    for slot in range(n_lon):
        @pl.when(has_up)
        def _():
            lat_f(0, slot).wait_send()

        @pl.when(has_down)
        def _():
            lat_f(1, slot).wait_send()

    @pl.when(has_up)
    def _():
        send_g(0).wait_send()

    @pl.when(has_down)
    def _():
        send_g(1).wait_send()

    for g in range(groups):
        send_p(g).wait_send()
        for step in range(1, chips):
            send_x(g, step).wait_send()
        send_q(g).wait_send()


def body(fields, upstream, weights, filter_taps, cycle_counts, cycle_blocks):
    channels, _, width = fields.shape
    kernels = weights.shape[0]
    n_lat, n_lon = lax.axis_size("lat"), lax.axis_size("lon")
    chunk = channels // n_lon
    groups = kernels // 3 if kernels % 3 == 0 else kernels
    rows, half = kernels // groups * chunk, channels // 2
    bf16, f32 = jnp.bfloat16, jnp.float32
    dma = pltpu.SemaphoreType.DMA
    vmem = pl.BlockSpec(memory_space=pltpu.VMEM)
    smem = pl.BlockSpec(memory_space=pltpu.SMEM)
    anywhere = pl.BlockSpec(memory_space=pl.ANY)
    results = pl.pallas_call(
        functools.partial(kernel, n_lat, n_lon),
        out_shape=(
            jax.ShapeDtypeStruct((channels, width), bf16),
            jax.ShapeDtypeStruct((channels, width), bf16),
            jax.ShapeDtypeStruct((kernels * chunk, channels), f32),
        ),
        in_specs=[vmem, smem, smem, vmem, vmem, anywhere],
        out_specs=[vmem] * 3,
        scratch_shapes=[
            pltpu.VMEM(weights.shape, bf16),
            pltpu.VMEM((kernels * channels, channels), bf16),
            pltpu.VMEM((width, channels), bf16),
            pltpu.VMEM((n_lon, 3, width, channels), bf16),
            pltpu.VMEM((n_lon, channels, width), bf16),
            pltpu.VMEM((n_lon, chunk, width), bf16),
            pltpu.VMEM((kernels * width, 9 * width), bf16),
            pltpu.VMEM((kernels, n_lon, width, channels), bf16),
            pltpu.VMEM((3, channels, kernels * width), bf16),
            pltpu.VMEM((3, channels, width), f32),
            pltpu.VMEM((2, channels, width), f32),
            pltpu.VMEM((2, groups, rows, half), f32),
            pltpu.VMEM((groups, rows, half), f32),
            pltpu.VMEM((n_lat // 2, groups, rows, half), bf16),
            pltpu.VMEM((2, groups, rows, half), f32),
            dma((n_lon,)), dma((n_lon,)), dma((n_lon,)), dma((n_lon,)), dma((n_lon,)), dma((n_lon,)),
            dma((2, n_lon)), dma((2, n_lon)), dma((2,)), dma((2,)),
            dma((groups,)), dma((groups,)), dma((groups, n_lat // 2)), dma((groups, n_lat // 2 + 1)),
            dma((groups,)), dma((groups,)), dma,
        ],
        compiler_params=pltpu.CompilerParams(
            collective_id=0, has_side_effects=True, vmem_limit_bytes=56 * 1024 * 1024
        ),
        cost_estimate=pl.CostEstimate(
            flops=8_000_000_000, bytes_accessed=3_000_000, transcendentals=0
        ),
    )(
        filter_taps, cycle_counts, cycle_blocks,
        fields.reshape(channels, width), upstream.reshape(channels, width), weights,
    )
    outputs, grad, weight_grad = pl.pallas_call(
        finish,
        out_shape=tuple(jax.ShapeDtypeStruct(held.shape, held.dtype) for held in results),
        in_specs=[vmem] * 3,
        out_specs=[vmem] * 3,
    )(*results)
    return (
        outputs.reshape(fields.shape),
        grad.reshape(fields.shape),
        weight_grad.reshape(kernels, chunk, channels),
    )


def solution(mesh):
    return jax.shard_map(
        body,
        mesh=mesh,
        in_specs=(
            P("groups", "lat", "lon"),
            P("groups", "lat", "lon"),
            P(),
            P("lat", None, None, None, None),
            P("lat"),
            P("lat", None),
        ),
        out_specs=(P("groups", "lat", "lon"), P("groups", "lat", "lon"), P("groups", "lon", None)),
        check_vma=False,
    )
```

```python
import functools

import jax
import jax.numpy as jnp
from jax import lax
from jax.experimental import pallas as pl
from jax.experimental.pallas import tpu as pltpu
from jax.sharding import PartitionSpec as P

HALO = 128
MESH = pl.DeviceIdType.MESH


def finish(*refs):
    count = len(refs) // 2
    for i in range(count):
        refs[count + i][...] = refs[i][...]


def kernel(
    n_lat, n_lon, taps_ref, counts_ref, blocks_ref, f_ref, u_ref, w_hbm, out_ref, grad_ref, wg_ref,
    w_ref, w_turned, f_mine, f_all, u_all, u_chunk, band, resp, met, rg, g_mine, g_got,
    part, part_got, chip, result,
    zf_s, zf_r, zc_s, zc_r, zu_s, zu_r, lf_s, lf_r, g_s, g_r, p_s, p_r, x_s, x_r, q_s, q_r, w_s,
):
    kernels, channels, _ = w_ref.shape
    width = f_ref.shape[1]
    chunk = u_chunk.shape[1]
    chips = n_lat // 2
    a = lax.axis_index("lat")
    b = lax.axis_index("lon")
    core = lax.rem(a, 2)
    chip_at = a // 2
    twin = a + 1 - 2 * core
    has_up = a < n_lat - 1
    has_down = a > 0

    def lon_peer(step):
        return {"lat": a, "lon": lax.rem(b + step, n_lon)}

    def lat_peer(at):
        return {"lat": at, "lon": b}

    load_w = pltpu.make_async_copy(w_hbm, w_ref, w_s)
    load_w.start()
    barrier = pltpu.get_barrier_semaphore()
    for step in range(1, n_lon):
        pl.semaphore_signal(barrier, inc=1, device_id=lon_peer(step), device_id_type=MESH)
    for step in range(1, n_lat):
        pl.semaphore_signal(
            barrier, inc=1, device_id=lat_peer(lax.rem(a + step, n_lat)), device_id_type=MESH
        )
    f_mine[...] = f_ref[...].T
    pl.semaphore_wait(barrier, n_lon + n_lat - 2)

    def remote(src, dst, send, recv, to):
        return pltpu.make_async_remote_copy(
            src_ref=src, dst_ref=dst, send_sem=send, recv_sem=recv, device_id=to,
            device_id_type=MESH,
        )

    def send_f(step):
        slot = n_lon - step
        return remote(f_mine, f_all.at[slot, 1], zf_s.at[step], zf_r.at[slot], lon_peer(step))

    def send_chunk(step):
        slot = n_lon - step
        start = pl.multiple_of(lax.rem(b + step, n_lon) * chunk, chunk)
        return remote(
            u_ref.at[pl.ds(start, chunk)], u_chunk.at[slot], zc_s.at[step], zc_r.at[slot],
            lon_peer(step),
        )

    def send_u(step):
        slot = n_lon - step
        return remote(u_ref, u_all.at[slot], zu_s.at[step], zu_r.at[slot], lon_peer(step))

    def lat_f(way, slot):
        to = a + 1 if way == 0 else a - 1
        src = f_mine if slot == 0 else f_all.at[slot, 1]
        return remote(
            src, f_all.at[slot, 2 * way], lf_s.at[way, slot], lf_r.at[way, slot], lat_peer(to)
        )

    steps = sorted(range(1, n_lon), key=lambda step: min(step, n_lon - step))
    for step in steps:
        send_chunk(step).start()
    for step in steps:
        send_f(step).start()

    @pl.when(has_up)
    def _():
        lat_f(0, 0).start()

    @pl.when(has_down)
    def _():
        lat_f(1, 0).start()

    slots, block_width = taps_ref.shape[3:]
    lane = lax.broadcasted_iota(jnp.int32, (slots, 4 * HALO), 1)
    which = lax.broadcasted_iota(jnp.int32, (slots, 4 * HALO), 0)
    first = jnp.zeros((slots, 4 * HALO), jnp.int32)
    for s in range(slots):
        first = jnp.where(which == s, HALO + block_width * blocks_ref[0, s], first)
    used = (which < counts_ref[0]) & (lane >= first) & (lane < first + block_width)
    rest = jnp.zeros((slots, 2 * HALO), jnp.float32)
    for k in range(kernels):
        for r in range(3):
            tile = taps_ref[0, k, r].astype(jnp.float32)
            spread = jnp.concatenate([tile] * (2 * HALO // block_width) + [rest], axis=1)
            row = jnp.sum(jnp.where(used, spread, 0.0), axis=0, keepdims=True)
            turned = pltpu.roll(
                jnp.broadcast_to(row, (width, 4 * HALO)), 0, 1, stride=1, stride_axis=0
            ).astype(jnp.bfloat16)
            for d in range(3):
                band[k * width : (k + 1) * width, (3 * d + r) * width : (3 * d + r + 1) * width] = (
                    turned[:, d * width : (d + 1) * width]
                )

    f_all[0, 1] = f_mine[...]

    @pl.when(jnp.logical_not(has_down))
    def _():
        f_all[:, 0] = jnp.zeros((n_lon, width, channels), f_all.dtype)

    @pl.when(jnp.logical_not(has_up))
    def _():
        f_all[:, 2] = jnp.zeros((n_lon, width, channels), f_all.dtype)

    u_chunk[0] = u_ref[pl.ds(pl.multiple_of(b * chunk, chunk), chunk), :]
    for step in steps:
        send_chunk(step).wait_recv()
    lines = jnp.concatenate(
        [
            jnp.concatenate([u_chunk[(slot + 1 - d) % n_lon] for d in range(3)], axis=1)
            for slot in range(n_lon)
        ],
        axis=0,
    )
    for k in range(kernels):
        rows = slice(k * width, (k + 1) * width)
        taps_k = jnp.concatenate(
            [band[rows, 3 * d * width : 3 * (d + 1) * width] for d in range(3)], axis=0
        )
        spread = jnp.dot(lines, taps_k, preferred_element_type=jnp.float32).astype(jnp.bfloat16)
        for slot in range(n_lon):
            met[slot, k * chunk : (k + 1) * chunk, :] = spread[slot * chunk : (slot + 1) * chunk]

    for step in steps:
        slot = n_lon - step
        send_f(step).wait_recv()

        @pl.when(has_up)
        def _():
            lat_f(0, slot).start()

        @pl.when(has_down)
        def _():
            lat_f(1, slot).start()

    for step in (1, n_lon - 1):
        send_u(step).start()

    load_w.wait()
    for k in range(kernels):
        w_turned[k * channels : (k + 1) * channels, :] = w_ref[k].T

    def wait_lat(slot):
        @pl.when(has_down)
        def _():
            lat_f(0, slot).wait_recv()

        @pl.when(has_up)
        def _():
            lat_f(1, slot).wait_recv()

    group = 3 if kernels % 3 == 0 else 1
    groups = kernels // group

    order = [0] + [n_lon - step for step in steps]
    total = jnp.zeros((kernels * chunk, channels), jnp.float32)
    for slot in order[:-1]:
        wait_lat(slot)
        total = total + jnp.dot(
            met[slot], f_all[slot].reshape(3 * width, channels),
            preferred_element_type=jnp.float32,
        )
    for g in range(groups):
        for half in range(2):
            part[half, g] = total[
                g * group * chunk : (g + 1) * group * chunk,
                half * channels // 2 : (half + 1) * channels // 2,
            ]
    wait_lat(order[-1])

    def send_p(g):
        return remote(
            part.at[1 - core, g], part_got.at[g], p_s.at[g], p_r.at[g], lat_peer(twin)
        )

    for g in range(groups):
        piece = jnp.dot(
            met[order[-1], g * group * chunk : (g + 1) * group * chunk, :],
            f_all[order[-1]].reshape(3 * width, channels),
            preferred_element_type=jnp.float32,
        )
        for half in range(2):
            part[half, g] += piece[:, half * channels // 2 : (half + 1) * channels // 2]
        send_p(g).start()

    window = jnp.concatenate(
        [f_all[slot].reshape(3 * width, channels) for slot in (n_lon - 1, 0, 1)], axis=0
    )

    def convolve(g):
        got = jnp.dot(
            band[g * group * width : (g + 1) * group * width, :], window,
            preferred_element_type=jnp.float32,
        ).astype(jnp.bfloat16)
        for k in range(group):
            resp[:, (g * group + k) * channels : (g * group + k + 1) * channels] = got[
                k * width : (k + 1) * width
            ]

    def send_x(g, step):
        to = lax.rem(a + 2 * step, n_lat)
        return remote(
            chip.at[chip_at, g], chip.at[chip_at, g], x_s.at[g, step],
            x_r.at[g, chips - step], lat_peer(to),
        )

    def got_x(g, step):
        at = lax.rem(chip_at + chips - step, chips)
        return remote(
            chip.at[at, g], chip.at[at, g], x_s.at[g, step], x_r.at[g, chips - step],
            lat_peer(twin),
        )

    for g in range(groups):
        convolve(g)
        send_p(g).wait_recv()
        chip[chip_at, g] = (part[core, g] + part_got[g]).astype(chip.dtype)
        for step in range(1, chips):
            send_x(g, step).start()

    u_all[0] = u_ref[...]
    for step in (1, n_lon - 1):
        send_u(step).wait_recv()
    u_wide = jnp.concatenate([u_all[n_lon - 1], u_all[0], u_all[1]], axis=1)
    for k in range(kernels):
        mixed = jnp.dot(
            w_turned[k * channels : (k + 1) * channels, :], u_wide,
            preferred_element_type=jnp.float32,
        ).astype(jnp.bfloat16)
        for j in range(3):
            rg[j, :, k * width : (k + 1) * width] = mixed[:, j * width : (j + 1) * width]
    terms = jnp.zeros((channels, 3 * width), jnp.float32)
    for j in range(3):
        terms = terms + jnp.dot(
            rg[j], band[:, (2 - j) * 3 * width : (3 - j) * 3 * width],
            preferred_element_type=jnp.float32,
        )
    for r in range(3):
        g_mine[r] = terms[:, r * width : (r + 1) * width]

    def send_g(way):
        to = a + 1 if way == 0 else a - 1
        return remote(g_mine.at[2 - 2 * way], g_got.at[way], g_s.at[way], g_r.at[way], lat_peer(to))

    @pl.when(has_up)
    def _():
        send_g(0).start()

    @pl.when(has_down)
    def _():
        send_g(1).start()

    mixed = jnp.dot(resp[...], w_turned[...], preferred_element_type=jnp.float32)
    out_ref[...] = mixed.astype(out_ref.dtype).T

    def send_q(g):
        return remote(result.at[core, g], result.at[core, g], q_s.at[g], q_r.at[g], lat_peer(twin))

    def got_q(g):
        return remote(
            result.at[1 - core, g], result.at[1 - core, g], q_s.at[g], q_r.at[g], lat_peer(twin)
        )

    for g in range(groups):
        for step in range(1, chips):
            got_x(g, step).wait_recv()
        total = chip[0, g].astype(jnp.float32)
        for at in range(1, chips):
            total = total + chip[at, g].astype(jnp.float32)
        result[core, g] = total
        send_q(g).start()

    @pl.when(has_down)
    def _():
        send_g(0).wait_recv()

    @pl.when(has_up)
    def _():
        send_g(1).wait_recv()

    below = jnp.where(has_down, g_got[0], 0.0)
    above = jnp.where(has_up, g_got[1], 0.0)
    grad_ref[...] = (g_mine[1] + below + above).astype(grad_ref.dtype)

    for g in range(groups):
        got_q(g).wait_recv()
        rows = slice(g * group * chunk, (g + 1) * group * chunk)
        wg_ref[rows, : channels // 2] = result[0, g]
        wg_ref[rows, channels // 2 :] = result[1, g]

    for step in range(1, n_lon):
        send_f(step).wait_send()
        send_chunk(step).wait_send()
    for step in (1, n_lon - 1):
        send_u(step).wait_send()
    for slot in range(n_lon):
        @pl.when(has_up)
        def _():
            lat_f(0, slot).wait_send()

        @pl.when(has_down)
        def _():
            lat_f(1, slot).wait_send()

    @pl.when(has_up)
    def _():
        send_g(0).wait_send()

    @pl.when(has_down)
    def _():
        send_g(1).wait_send()

    for g in range(groups):
        send_p(g).wait_send()
        for step in range(1, chips):
            send_x(g, step).wait_send()
        send_q(g).wait_send()


def body(fields, upstream, weights, filter_taps, cycle_counts, cycle_blocks):
    channels, _, width = fields.shape
    kernels = weights.shape[0]
    n_lat, n_lon = lax.axis_size("lat"), lax.axis_size("lon")
    chunk = channels // n_lon
    groups = kernels // 3 if kernels % 3 == 0 else kernels
    rows, half = kernels // groups * chunk, channels // 2
    bf16, f32 = jnp.bfloat16, jnp.float32
    dma = pltpu.SemaphoreType.DMA
    vmem = pl.BlockSpec(memory_space=pltpu.VMEM)
    smem = pl.BlockSpec(memory_space=pltpu.SMEM)
    anywhere = pl.BlockSpec(memory_space=pl.ANY)
    results = pl.pallas_call(
        functools.partial(kernel, n_lat, n_lon),
        out_shape=(
            jax.ShapeDtypeStruct((channels, width), bf16),
            jax.ShapeDtypeStruct((channels, width), bf16),
            jax.ShapeDtypeStruct((kernels * chunk, channels), f32),
        ),
        in_specs=[vmem, smem, smem, vmem, vmem, anywhere],
        out_specs=[vmem] * 3,
        scratch_shapes=[
            pltpu.VMEM(weights.shape, bf16),
            pltpu.VMEM((kernels * channels, channels), bf16),
            pltpu.VMEM((width, channels), bf16),
            pltpu.VMEM((n_lon, 3, width, channels), bf16),
            pltpu.VMEM((n_lon, channels, width), bf16),
            pltpu.VMEM((n_lon, chunk, width), bf16),
            pltpu.VMEM((kernels * width, 9 * width), bf16),
            pltpu.VMEM((width, kernels * channels), bf16),
            pltpu.VMEM((n_lon, kernels * chunk, 3 * width), bf16),
            pltpu.VMEM((3, channels, kernels * width), bf16),
            pltpu.VMEM((3, channels, width), f32),
            pltpu.VMEM((2, channels, width), f32),
            pltpu.VMEM((2, groups, rows, half), f32),
            pltpu.VMEM((groups, rows, half), f32),
            pltpu.VMEM((n_lat // 2, groups, rows, half), bf16),
            pltpu.VMEM((2, groups, rows, half), f32),
            dma((n_lon,)), dma((n_lon,)), dma((n_lon,)), dma((n_lon,)), dma((n_lon,)), dma((n_lon,)),
            dma((2, n_lon)), dma((2, n_lon)), dma((2,)), dma((2,)),
            dma((groups,)), dma((groups,)), dma((groups, n_lat // 2)), dma((groups, n_lat // 2 + 1)),
            dma((groups,)), dma((groups,)), dma,
        ],
        compiler_params=pltpu.CompilerParams(
            collective_id=0, has_side_effects=True, vmem_limit_bytes=56 * 1024 * 1024
        ),
        cost_estimate=pl.CostEstimate(
            flops=8_000_000_000, bytes_accessed=3_000_000, transcendentals=0
        ),
    )(
        filter_taps, cycle_counts, cycle_blocks,
        fields.reshape(channels, width), upstream.reshape(channels, width), weights,
    )
    outputs, grad, weight_grad = pl.pallas_call(
        finish,
        out_shape=tuple(jax.ShapeDtypeStruct(held.shape, held.dtype) for held in results),
        in_specs=[vmem] * 3,
        out_specs=[vmem] * 3,
    )(*results)
    return (
        outputs.reshape(fields.shape),
        grad.reshape(fields.shape),
        weight_grad.reshape(kernels, chunk, channels),
    )


def solution(mesh):
    return jax.shard_map(
        body,
        mesh=mesh,
        in_specs=(
            P("groups", "lat", "lon"),
            P("groups", "lat", "lon"),
            P(),
            P("lat", None, None, None, None),
            P("lat"),
            P("lat", None),
        ),
        out_specs=(P("groups", "lat", "lon"), P("groups", "lat", "lon"), P("groups", "lon", None)),
        check_vma=False,
    )
```

```python
import functools

import jax
import jax.numpy as jnp
from jax import lax
from jax.experimental import pallas as pl
from jax.experimental.pallas import tpu as pltpu
from jax.sharding import PartitionSpec as P

HALO = 128
MESH = pl.DeviceIdType.MESH


def finish(*refs):
    count = len(refs) // 2
    for i in range(count):
        refs[count + i][...] = refs[i][...]


def kernel(
    n_lat, n_lon, taps_ref, counts_ref, blocks_ref, f_ref, u_ref, w_hbm, out_ref, grad_ref, wg_ref,
    w_ref, w_turned, f_mine, f_all, u_all, u_chunk, band, resp, met, rg, g_mine, g_got,
    part, part_got, chip, result,
    zf_s, zf_r, zc_s, zc_r, zu_s, zu_r, lf_s, lf_r, g_s, g_r, p_s, p_r, x_s, x_r, q_s, q_r, w_s,
):
    kernels, channels, _ = w_ref.shape
    width = f_ref.shape[1]
    chunk = u_chunk.shape[1]
    chips = n_lat // 2
    a = lax.axis_index("lat")
    b = lax.axis_index("lon")
    core = lax.rem(a, 2)
    chip_at = a // 2
    twin = a + 1 - 2 * core
    has_up = a < n_lat - 1
    has_down = a > 0

    def lon_peer(step):
        return {"lat": a, "lon": lax.rem(b + step, n_lon)}

    def lat_peer(at):
        return {"lat": at, "lon": b}

    load_w = pltpu.make_async_copy(w_hbm, w_ref, w_s)
    load_w.start()
    barrier = pltpu.get_barrier_semaphore()
    for step in range(1, n_lon):
        pl.semaphore_signal(barrier, inc=1, device_id=lon_peer(step), device_id_type=MESH)
    for step in range(1, n_lat):
        pl.semaphore_signal(
            barrier, inc=1, device_id=lat_peer(lax.rem(a + step, n_lat)), device_id_type=MESH
        )
    f_mine[...] = f_ref[...].T
    pl.semaphore_wait(barrier, n_lon + n_lat - 2)

    def remote(src, dst, send, recv, to):
        return pltpu.make_async_remote_copy(
            src_ref=src, dst_ref=dst, send_sem=send, recv_sem=recv, device_id=to,
            device_id_type=MESH,
        )

    def send_f(step):
        slot = n_lon - step
        return remote(f_mine, f_all.at[slot, 1], zf_s.at[step], zf_r.at[slot], lon_peer(step))

    def send_chunk(step):
        slot = n_lon - step
        start = pl.multiple_of(lax.rem(b + step, n_lon) * chunk, chunk)
        return remote(
            u_ref.at[pl.ds(start, chunk)], u_chunk.at[slot], zc_s.at[step], zc_r.at[slot],
            lon_peer(step),
        )

    def send_u(step):
        slot = n_lon - step
        return remote(u_ref, u_all.at[slot], zu_s.at[step], zu_r.at[slot], lon_peer(step))

    def lat_f(way, slot):
        to = a + 1 if way == 0 else a - 1
        src = f_mine if slot == 0 else f_all.at[slot, 1]
        return remote(
            src, f_all.at[slot, 2 * way], lf_s.at[way, slot], lf_r.at[way, slot], lat_peer(to)
        )

    steps = sorted(range(1, n_lon), key=lambda step: min(step, n_lon - step))
    for step in steps:
        send_chunk(step).start()
    for step in steps:
        send_f(step).start()

    @pl.when(has_up)
    def _():
        lat_f(0, 0).start()

    @pl.when(has_down)
    def _():
        lat_f(1, 0).start()

    slots, block_width = taps_ref.shape[3:]
    lane = lax.broadcasted_iota(jnp.int32, (slots, 4 * HALO), 1)
    which = lax.broadcasted_iota(jnp.int32, (slots, 4 * HALO), 0)
    first = jnp.zeros((slots, 4 * HALO), jnp.int32)
    for s in range(slots):
        first = jnp.where(which == s, HALO + block_width * blocks_ref[0, s], first)
    used = (which < counts_ref[0]) & (lane >= first) & (lane < first + block_width)
    rest = jnp.zeros((slots, 2 * HALO), jnp.float32)
    for k in range(kernels):
        for r in range(3):
            tile = taps_ref[0, k, r].astype(jnp.float32)
            spread = jnp.concatenate([tile] * (2 * HALO // block_width) + [rest], axis=1)
            row = jnp.sum(jnp.where(used, spread, 0.0), axis=0, keepdims=True)
            eight = pltpu.roll(
                jnp.broadcast_to(row, (8, 4 * HALO)), 0, 1, stride=1, stride_axis=0
            )
            turned = jnp.concatenate(
                [eight if p == 0 else pltpu.roll(eight, p, 1) for p in range(0, width, 8)], axis=0
            ).astype(jnp.bfloat16)
            for d in range(3):
                band[k * width : (k + 1) * width, (3 * d + r) * width : (3 * d + r + 1) * width] = (
                    turned[:, d * width : (d + 1) * width]
                )

    f_all[0, 1] = f_mine[...]

    @pl.when(jnp.logical_not(has_down))
    def _():
        f_all[:, 0] = jnp.zeros((n_lon, width, channels), f_all.dtype)

    @pl.when(jnp.logical_not(has_up))
    def _():
        f_all[:, 2] = jnp.zeros((n_lon, width, channels), f_all.dtype)

    for step in steps:
        slot = n_lon - step
        send_f(step).wait_recv()

        @pl.when(has_up)
        def _():
            lat_f(0, slot).start()

        @pl.when(has_down)
        def _():
            lat_f(1, slot).start()

    for step in (1, n_lon - 1):
        send_u(step).start()

    u_chunk[0] = u_ref[pl.ds(pl.multiple_of(b * chunk, chunk), chunk), :]
    for step in steps:
        send_chunk(step).wait_recv()
    lines = jnp.concatenate(
        [
            jnp.concatenate([u_chunk[(slot + 1 - d) % n_lon] for d in range(3)], axis=1)
            for slot in range(n_lon)
        ],
        axis=0,
    )
    for k in range(kernels):
        rows = slice(k * width, (k + 1) * width)
        taps_k = jnp.concatenate(
            [band[rows, 3 * d * width : 3 * (d + 1) * width] for d in range(3)], axis=0
        )
        spread = jnp.dot(lines, taps_k, preferred_element_type=jnp.float32).astype(jnp.bfloat16)
        for slot in range(n_lon):
            met[slot, k * chunk : (k + 1) * chunk, :] = spread[slot * chunk : (slot + 1) * chunk]

    load_w.wait()
    for k in range(kernels):
        w_turned[k * channels : (k + 1) * channels, :] = w_ref[k].T

    def wait_lat(slot):
        @pl.when(has_down)
        def _():
            lat_f(0, slot).wait_recv()

        @pl.when(has_up)
        def _():
            lat_f(1, slot).wait_recv()

    group = 3 if kernels % 3 == 0 else 1
    groups = kernels // group

    order = [0] + [n_lon - step for step in steps]
    total = jnp.zeros((kernels * chunk, channels), jnp.float32)
    for slot in order[:-1]:
        wait_lat(slot)
        total = total + jnp.dot(
            met[slot], f_all[slot].reshape(3 * width, channels),
            preferred_element_type=jnp.float32,
        )
    for g in range(groups):
        for half in range(2):
            part[half, g] = total[
                g * group * chunk : (g + 1) * group * chunk,
                half * channels // 2 : (half + 1) * channels // 2,
            ]
    wait_lat(order[-1])

    def send_p(g):
        return remote(
            part.at[1 - core, g], part_got.at[g], p_s.at[g], p_r.at[g], lat_peer(twin)
        )

    for g in range(groups):
        piece = jnp.dot(
            met[order[-1], g * group * chunk : (g + 1) * group * chunk, :],
            f_all[order[-1]].reshape(3 * width, channels),
            preferred_element_type=jnp.float32,
        )
        for half in range(2):
            part[half, g] += piece[:, half * channels // 2 : (half + 1) * channels // 2]
        send_p(g).start()

    window = jnp.concatenate(
        [f_all[slot].reshape(3 * width, channels) for slot in (n_lon - 1, 0, 1)], axis=0
    )

    def convolve(g):
        got = jnp.dot(
            band[g * group * width : (g + 1) * group * width, :], window,
            preferred_element_type=jnp.float32,
        ).astype(jnp.bfloat16)
        for k in range(group):
            resp[:, (g * group + k) * channels : (g * group + k + 1) * channels] = got[
                k * width : (k + 1) * width
            ]

    def send_x(g, step):
        to = lax.rem(a + 2 * step, n_lat)
        return remote(
            chip.at[chip_at, g], chip.at[chip_at, g], x_s.at[g, step],
            x_r.at[g, chips - step], lat_peer(to),
        )

    def got_x(g, step):
        at = lax.rem(chip_at + chips - step, chips)
        return remote(
            chip.at[at, g], chip.at[at, g], x_s.at[g, step], x_r.at[g, chips - step],
            lat_peer(twin),
        )

    for g in range(groups):
        convolve(g)
        send_p(g).wait_recv()
        chip[chip_at, g] = (part[core, g] + part_got[g]).astype(chip.dtype)
        for step in range(1, chips):
            send_x(g, step).start()

    u_all[0] = u_ref[...]
    for step in (1, n_lon - 1):
        send_u(step).wait_recv()
    u_wide = jnp.concatenate([u_all[n_lon - 1], u_all[0], u_all[1]], axis=1)
    for k in range(kernels):
        mixed = jnp.dot(
            w_turned[k * channels : (k + 1) * channels, :], u_wide,
            preferred_element_type=jnp.float32,
        ).astype(jnp.bfloat16)
        for j in range(3):
            rg[j, :, k * width : (k + 1) * width] = mixed[:, j * width : (j + 1) * width]
    terms = jnp.zeros((channels, 3 * width), jnp.float32)
    for j in range(3):
        terms = terms + jnp.dot(
            rg[j], band[:, (2 - j) * 3 * width : (3 - j) * 3 * width],
            preferred_element_type=jnp.float32,
        )
    for r in range(3):
        g_mine[r] = terms[:, r * width : (r + 1) * width]

    def send_g(way):
        to = a + 1 if way == 0 else a - 1
        return remote(g_mine.at[2 - 2 * way], g_got.at[way], g_s.at[way], g_r.at[way], lat_peer(to))

    @pl.when(has_up)
    def _():
        send_g(0).start()

    @pl.when(has_down)
    def _():
        send_g(1).start()

    mixed = jnp.dot(resp[...], w_turned[...], preferred_element_type=jnp.float32)
    out_ref[...] = mixed.astype(out_ref.dtype).T

    def send_q(g):
        return remote(result.at[core, g], result.at[core, g], q_s.at[g], q_r.at[g], lat_peer(twin))

    def got_q(g):
        return remote(
            result.at[1 - core, g], result.at[1 - core, g], q_s.at[g], q_r.at[g], lat_peer(twin)
        )

    for g in range(groups):
        for step in range(1, chips):
            got_x(g, step).wait_recv()
        total = chip[0, g].astype(jnp.float32)
        for at in range(1, chips):
            total = total + chip[at, g].astype(jnp.float32)
        result[core, g] = total
        send_q(g).start()

    @pl.when(has_down)
    def _():
        send_g(0).wait_recv()

    @pl.when(has_up)
    def _():
        send_g(1).wait_recv()

    below = jnp.where(has_down, g_got[0], 0.0)
    above = jnp.where(has_up, g_got[1], 0.0)
    grad_ref[...] = (g_mine[1] + below + above).astype(grad_ref.dtype)

    for g in range(groups):
        got_q(g).wait_recv()
        rows = slice(g * group * chunk, (g + 1) * group * chunk)
        wg_ref[rows, : channels // 2] = result[0, g]
        wg_ref[rows, channels // 2 :] = result[1, g]

    for step in range(1, n_lon):
        send_f(step).wait_send()
        send_chunk(step).wait_send()
    for step in (1, n_lon - 1):
        send_u(step).wait_send()
    for slot in range(n_lon):
        @pl.when(has_up)
        def _():
            lat_f(0, slot).wait_send()

        @pl.when(has_down)
        def _():
            lat_f(1, slot).wait_send()

    @pl.when(has_up)
    def _():
        send_g(0).wait_send()

    @pl.when(has_down)
    def _():
        send_g(1).wait_send()

    for g in range(groups):
        send_p(g).wait_send()
        for step in range(1, chips):
            send_x(g, step).wait_send()
        send_q(g).wait_send()


def body(fields, upstream, weights, filter_taps, cycle_counts, cycle_blocks):
    channels, _, width = fields.shape
    kernels = weights.shape[0]
    n_lat, n_lon = lax.axis_size("lat"), lax.axis_size("lon")
    chunk = channels // n_lon
    groups = kernels // 3 if kernels % 3 == 0 else kernels
    rows, half = kernels // groups * chunk, channels // 2
    bf16, f32 = jnp.bfloat16, jnp.float32
    dma = pltpu.SemaphoreType.DMA
    vmem = pl.BlockSpec(memory_space=pltpu.VMEM)
    smem = pl.BlockSpec(memory_space=pltpu.SMEM)
    anywhere = pl.BlockSpec(memory_space=pl.ANY)
    results = pl.pallas_call(
        functools.partial(kernel, n_lat, n_lon),
        out_shape=(
            jax.ShapeDtypeStruct((channels, width), bf16),
            jax.ShapeDtypeStruct((channels, width), bf16),
            jax.ShapeDtypeStruct((kernels * chunk, channels), f32),
        ),
        in_specs=[vmem, smem, smem, vmem, vmem, anywhere],
        out_specs=[vmem] * 3,
        scratch_shapes=[
            pltpu.VMEM(weights.shape, bf16),
            pltpu.VMEM((kernels * channels, channels), bf16),
            pltpu.VMEM((width, channels), bf16),
            pltpu.VMEM((n_lon, 3, width, channels), bf16),
            pltpu.VMEM((n_lon, channels, width), bf16),
            pltpu.VMEM((n_lon, chunk, width), bf16),
            pltpu.VMEM((kernels * width, 9 * width), bf16),
            pltpu.VMEM((width, kernels * channels), bf16),
            pltpu.VMEM((n_lon, kernels * chunk, 3 * width), bf16),
            pltpu.VMEM((3, channels, kernels * width), bf16),
            pltpu.VMEM((3, channels, width), f32),
            pltpu.VMEM((2, channels, width), f32),
            pltpu.VMEM((2, groups, rows, half), f32),
            pltpu.VMEM((groups, rows, half), f32),
            pltpu.VMEM((n_lat // 2, groups, rows, half), bf16),
            pltpu.VMEM((2, groups, rows, half), f32),
            dma((n_lon,)), dma((n_lon,)), dma((n_lon,)), dma((n_lon,)), dma((n_lon,)), dma((n_lon,)),
            dma((2, n_lon)), dma((2, n_lon)), dma((2,)), dma((2,)),
            dma((groups,)), dma((groups,)), dma((groups, n_lat // 2)), dma((groups, n_lat // 2 + 1)),
            dma((groups,)), dma((groups,)), dma,
        ],
        compiler_params=pltpu.CompilerParams(
            collective_id=0, has_side_effects=True, vmem_limit_bytes=(20 + n_lon) * 1024 * 1024
        ),
        cost_estimate=pl.CostEstimate(
            flops=8_000_000_000, bytes_accessed=3_000_000, transcendentals=0
        ),
    )(
        filter_taps, cycle_counts, cycle_blocks,
        fields.reshape(channels, width), upstream.reshape(channels, width), weights,
    )
    outputs, grad, weight_grad = pl.pallas_call(
        finish,
        out_shape=tuple(jax.ShapeDtypeStruct(held.shape, held.dtype) for held in results),
        in_specs=[vmem] * 3,
        out_specs=[vmem] * 3,
    )(*results)
    return (
        outputs.reshape(fields.shape),
        grad.reshape(fields.shape),
        weight_grad.reshape(kernels, chunk, channels),
    )


def solution(mesh):
    return jax.shard_map(
        body,
        mesh=mesh,
        in_specs=(
            P("groups", "lat", "lon"),
            P("groups", "lat", "lon"),
            P(),
            P("lat", None, None, None, None),
            P("lat"),
            P("lat", None),
        ),
        out_specs=(P("groups", "lat", "lon"), P("groups", "lat", "lon"), P("groups", "lon", None)),
        check_vma=False,
    )
```

```python
import functools

import jax
import jax.numpy as jnp
from jax import lax
from jax.experimental import pallas as pl
from jax.experimental.pallas import tpu as pltpu
from jax.sharding import PartitionSpec as P

HALO = 128
MESH = pl.DeviceIdType.MESH


def finish(*refs):
    count = len(refs) // 2
    for i in range(count):
        refs[count + i][...] = refs[i][...]


def kernel(
    n_lat, n_lon, taps_ref, counts_ref, blocks_ref, f_ref, u_ref, w_hbm, out_ref, grad_ref, wg_ref,
    w_ref, w_turned, f_mine, f_all, u_all, u_chunk, band, resp, met, rg, g_mine, g_out, g_got,
    part, part_got, chip, result,
    zf_s, zf_r, zc_s, zc_r, zu_s, zu_r, lf_s, lf_r, g_s, g_r, p_s, p_r, x_s, x_r, q_s, q_r, w_s,
):
    kernels, channels, _ = w_ref.shape
    width = f_ref.shape[1]
    chunk = u_chunk.shape[1]
    chips = n_lat // 2
    a = lax.axis_index("lat")
    b = lax.axis_index("lon")
    core = lax.rem(a, 2)
    chip_at = a // 2
    twin = a + 1 - 2 * core
    has_up = a < n_lat - 1
    has_down = a > 0

    def lon_peer(step):
        return {"lat": a, "lon": lax.rem(b + step, n_lon)}

    def lat_peer(at):
        return {"lat": at, "lon": b}

    load_w = pltpu.make_async_copy(w_hbm, w_ref, w_s)
    load_w.start()
    barrier = pltpu.get_barrier_semaphore()
    for step in range(1, n_lon):
        pl.semaphore_signal(barrier, inc=1, device_id=lon_peer(step), device_id_type=MESH)
    for step in range(1, n_lat):
        pl.semaphore_signal(
            barrier, inc=1, device_id=lat_peer(lax.rem(a + step, n_lat)), device_id_type=MESH
        )
    f_mine[...] = f_ref[...].T
    pl.semaphore_wait(barrier, n_lon + n_lat - 2)

    def remote(src, dst, send, recv, to):
        return pltpu.make_async_remote_copy(
            src_ref=src, dst_ref=dst, send_sem=send, recv_sem=recv, device_id=to,
            device_id_type=MESH,
        )

    def hop_f(way, t):
        slot = ((n_lon - (t - 1)) if way == 0 else (t - 1)) % n_lon
        lands = n_lon - t if way == 0 else t
        src = f_mine if t == 1 else f_all.at[slot, 1]
        to = {"lat": a, "lon": b + 1 if way == 0 else b - 1}
        return remote(src, f_all.at[lands, 1], zf_s.at[way, t], zf_r.at[lands], to)

    def hops_out(way, t):
        if way == 0:
            return (b + 1 < n_lon) & (b - t + 1 >= 0)
        return (b >= 1) & (b + t - 1 < n_lon)

    def hops_in(way, t):
        return b - t >= 0 if way == 0 else b + t < n_lon

    def start_hop(way, t):
        @pl.when(hops_out(way, t))
        def _():
            hop_f(way, t).start()

    def send_chunk(step):
        slot = n_lon - step
        start = pl.multiple_of(lax.rem(b + step, n_lon) * chunk, chunk)
        return remote(
            u_ref.at[pl.ds(start, chunk)], u_chunk.at[slot], zc_s.at[step], zc_r.at[slot],
            lon_peer(step),
        )

    def send_u(step):
        slot = n_lon - step
        return remote(u_ref, u_all.at[slot], zu_s.at[step], zu_r.at[slot], lon_peer(step))

    def lat_f(way, slot):
        to = a + 1 if way == 0 else a - 1
        src = f_mine if slot == 0 else f_all.at[slot, 1]
        return remote(
            src, f_all.at[slot, 2 * way], lf_s.at[way, slot], lf_r.at[way, slot], lat_peer(to)
        )

    steps = sorted(range(1, n_lon), key=lambda step: min(step, n_lon - step))
    for way in range(2):
        start_hop(way, 1)
    for step in steps:
        send_chunk(step).start()

    @pl.when(has_up)
    def _():
        lat_f(0, 0).start()

    @pl.when(has_down)
    def _():
        lat_f(1, 0).start()

    slots, block_width = taps_ref.shape[3:]
    lane = lax.broadcasted_iota(jnp.int32, (slots, 4 * HALO), 1)
    which = lax.broadcasted_iota(jnp.int32, (slots, 4 * HALO), 0)
    first = jnp.zeros((slots, 4 * HALO), jnp.int32)
    for s in range(slots):
        first = jnp.where(which == s, HALO + block_width * blocks_ref[0, s], first)
    used = (which < counts_ref[0]) & (lane >= first) & (lane < first + block_width)
    rest = jnp.zeros((slots, 2 * HALO), jnp.float32)
    for k in range(kernels):
        for r in range(3):
            tile = taps_ref[0, k, r].astype(jnp.float32)
            spread = jnp.concatenate([tile] * (2 * HALO // block_width) + [rest], axis=1)
            row = jnp.sum(jnp.where(used, spread, 0.0), axis=0, keepdims=True)
            eight = pltpu.roll(
                jnp.broadcast_to(row, (8, 4 * HALO)), 0, 1, stride=1, stride_axis=0
            )
            turned = jnp.concatenate(
                [eight if p == 0 else pltpu.roll(eight, p, 1) for p in range(0, width, 8)], axis=0
            ).astype(jnp.bfloat16)
            for d in range(3):
                band[k * width : (k + 1) * width, (3 * d + r) * width : (3 * d + r + 1) * width] = (
                    turned[:, d * width : (d + 1) * width]
                )

    f_all[0, 1] = f_mine[...]

    @pl.when(jnp.logical_not(has_down))
    def _():
        f_all[:, 0] = jnp.zeros((n_lon, width, channels), f_all.dtype)

    @pl.when(jnp.logical_not(has_up))
    def _():
        f_all[:, 2] = jnp.zeros((n_lon, width, channels), f_all.dtype)

    def pass_on(way, t):
        slot = n_lon - t if way == 0 else t

        @pl.when(hops_in(way, t))
        def _():
            hop_f(way, t).wait_recv()
            if t + 1 < n_lon:
                start_hop(way, t + 1)

            @pl.when(has_up)
            def _():
                lat_f(0, slot).start()

            @pl.when(has_down)
            def _():
                lat_f(1, slot).start()

    for t in range(1, n_lon):
        for way in range(2):
            pass_on(way, t)
        if t == 1:
            for step in (1, n_lon - 1):
                send_u(step).start()

    u_chunk[0] = u_ref[pl.ds(pl.multiple_of(b * chunk, chunk), chunk), :]
    for step in steps:
        send_chunk(step).wait_recv()
    lines = jnp.concatenate(
        [
            jnp.concatenate([u_chunk[(slot + 1 - d) % n_lon] for d in range(3)], axis=1)
            for slot in range(n_lon)
        ],
        axis=0,
    )
    for k in range(kernels):
        rows = slice(k * width, (k + 1) * width)
        taps_k = jnp.concatenate(
            [band[rows, 3 * d * width : 3 * (d + 1) * width] for d in range(3)], axis=0
        )
        spread = jnp.dot(lines, taps_k, preferred_element_type=jnp.float32).astype(jnp.bfloat16)
        for slot in range(n_lon):
            met[slot, k * chunk : (k + 1) * chunk, :] = spread[slot * chunk : (slot + 1) * chunk]

    load_w.wait()
    for k in range(kernels):
        w_turned[k * channels : (k + 1) * channels, :] = w_ref[k].T

    def wait_lat(slot):
        @pl.when(has_down)
        def _():
            lat_f(0, slot).wait_recv()

        @pl.when(has_up)
        def _():
            lat_f(1, slot).wait_recv()

    group = 3 if kernels % 3 == 0 else 1
    groups = kernels // group

    order = [0] + [n_lon - step for step in steps]
    total = jnp.zeros((kernels * chunk, channels), jnp.float32)
    for slot in order[:-1]:
        wait_lat(slot)
        total = total + jnp.dot(
            met[slot], f_all[slot].reshape(3 * width, channels),
            preferred_element_type=jnp.float32,
        )
    for g in range(groups):
        for half in range(2):
            part[half, g] = total[
                g * group * chunk : (g + 1) * group * chunk,
                half * channels // 2 : (half + 1) * channels // 2,
            ]
    wait_lat(order[-1])

    def send_p(g):
        return remote(
            part.at[1 - core, g], part_got.at[g], p_s.at[g], p_r.at[g], lat_peer(twin)
        )

    for g in range(groups):
        piece = jnp.dot(
            met[order[-1], g * group * chunk : (g + 1) * group * chunk, :],
            f_all[order[-1]].reshape(3 * width, channels),
            preferred_element_type=jnp.float32,
        )
        for half in range(2):
            part[half, g] += piece[:, half * channels // 2 : (half + 1) * channels // 2]
        send_p(g).start()

    window = jnp.concatenate(
        [f_all[slot].reshape(3 * width, channels) for slot in (n_lon - 1, 0, 1)], axis=0
    )

    def convolve(g):
        got = jnp.dot(
            band[g * group * width : (g + 1) * group * width, :], window,
            preferred_element_type=jnp.float32,
        ).astype(jnp.bfloat16)
        for k in range(group):
            resp[:, (g * group + k) * channels : (g * group + k + 1) * channels] = got[
                k * width : (k + 1) * width
            ]

    def send_x(g, step):
        to = lax.rem(a + 2 * step, n_lat)
        return remote(
            chip.at[chip_at, g], chip.at[chip_at, g], x_s.at[g, step],
            x_r.at[g, chips - step], lat_peer(to),
        )

    def got_x(g, step):
        at = lax.rem(chip_at + chips - step, chips)
        return remote(
            chip.at[at, g], chip.at[at, g], x_s.at[g, step], x_r.at[g, chips - step],
            lat_peer(twin),
        )

    for g in range(groups):
        convolve(g)
        send_p(g).wait_recv()
        chip[chip_at, g] = (part[core, g] + part_got[g]).astype(chip.dtype)
        for step in range(1, chips):
            send_x(g, step).start()

    u_all[0] = u_ref[...]
    for step in (1, n_lon - 1):
        send_u(step).wait_recv()
    u_wide = jnp.concatenate([u_all[n_lon - 1], u_all[0], u_all[1]], axis=1)
    for k in range(kernels):
        mixed = jnp.dot(
            w_turned[k * channels : (k + 1) * channels, :], u_wide,
            preferred_element_type=jnp.float32,
        ).astype(jnp.bfloat16)
        for j in range(3):
            rg[j, :, k * width : (k + 1) * width] = mixed[:, j * width : (j + 1) * width]
    terms = jnp.zeros((channels, 3 * width), jnp.float32)
    for j in range(3):
        terms = terms + jnp.dot(
            rg[j], band[:, (2 - j) * 3 * width : (3 - j) * 3 * width],
            preferred_element_type=jnp.float32,
        )
    g_mine[...] = terms[:, width : 2 * width]
    g_out[0] = terms[:, 2 * width :].astype(g_out.dtype)
    g_out[1] = terms[:, :width].astype(g_out.dtype)

    def send_g(way):
        to = a + 1 if way == 0 else a - 1
        return remote(g_out.at[way], g_got.at[way], g_s.at[way], g_r.at[way], lat_peer(to))

    @pl.when(has_up)
    def _():
        send_g(0).start()

    @pl.when(has_down)
    def _():
        send_g(1).start()

    mixed = jnp.dot(resp[...], w_turned[...], preferred_element_type=jnp.float32)
    out_ref[...] = mixed.astype(out_ref.dtype).T

    def send_q(g):
        return remote(result.at[core, g], result.at[core, g], q_s.at[g], q_r.at[g], lat_peer(twin))

    def got_q(g):
        return remote(
            result.at[1 - core, g], result.at[1 - core, g], q_s.at[g], q_r.at[g], lat_peer(twin)
        )

    for g in range(groups):
        for step in range(1, chips):
            got_x(g, step).wait_recv()
        total = chip[0, g].astype(jnp.float32)
        for at in range(1, chips):
            total = total + chip[at, g].astype(jnp.float32)
        result[core, g] = total
        send_q(g).start()

    @pl.when(has_down)
    def _():
        send_g(0).wait_recv()

    @pl.when(has_up)
    def _():
        send_g(1).wait_recv()

    below = jnp.where(has_down, g_got[0].astype(jnp.float32), 0.0)
    above = jnp.where(has_up, g_got[1].astype(jnp.float32), 0.0)
    grad_ref[...] = (g_mine[...] + below + above).astype(grad_ref.dtype)

    for g in range(groups):
        got_q(g).wait_recv()
        rows = slice(g * group * chunk, (g + 1) * group * chunk)
        wg_ref[rows, : channels // 2] = result[0, g]
        wg_ref[rows, channels // 2 :] = result[1, g]

    for step in range(1, n_lon):
        send_chunk(step).wait_send()
        for way in range(2):
            @pl.when(hops_out(way, step))
            def _():
                hop_f(way, step).wait_send()
    for step in (1, n_lon - 1):
        send_u(step).wait_send()
    for slot in range(n_lon):
        @pl.when(has_up)
        def _():
            lat_f(0, slot).wait_send()

        @pl.when(has_down)
        def _():
            lat_f(1, slot).wait_send()

    @pl.when(has_up)
    def _():
        send_g(0).wait_send()

    @pl.when(has_down)
    def _():
        send_g(1).wait_send()

    for g in range(groups):
        send_p(g).wait_send()
        for step in range(1, chips):
            send_x(g, step).wait_send()
        send_q(g).wait_send()


def body(fields, upstream, weights, filter_taps, cycle_counts, cycle_blocks):
    channels, _, width = fields.shape
    kernels = weights.shape[0]
    n_lat, n_lon = lax.axis_size("lat"), lax.axis_size("lon")
    chunk = channels // n_lon
    groups = kernels // 3 if kernels % 3 == 0 else kernels
    rows, half = kernels // groups * chunk, channels // 2
    bf16, f32 = jnp.bfloat16, jnp.float32
    dma = pltpu.SemaphoreType.DMA
    vmem = pl.BlockSpec(memory_space=pltpu.VMEM)
    smem = pl.BlockSpec(memory_space=pltpu.SMEM)
    anywhere = pl.BlockSpec(memory_space=pl.ANY)
    results = pl.pallas_call(
        functools.partial(kernel, n_lat, n_lon),
        out_shape=(
            jax.ShapeDtypeStruct((channels, width), bf16),
            jax.ShapeDtypeStruct((channels, width), bf16),
            jax.ShapeDtypeStruct((kernels * chunk, channels), f32),
        ),
        in_specs=[vmem, smem, smem, vmem, vmem, anywhere],
        out_specs=[vmem] * 3,
        scratch_shapes=[
            pltpu.VMEM(weights.shape, bf16),
            pltpu.VMEM((kernels * channels, channels), bf16),
            pltpu.VMEM((width, channels), bf16),
            pltpu.VMEM((n_lon, 3, width, channels), bf16),
            pltpu.VMEM((n_lon, channels, width), bf16),
            pltpu.VMEM((n_lon, chunk, width), bf16),
            pltpu.VMEM((kernels * width, 9 * width), bf16),
            pltpu.VMEM((width, kernels * channels), bf16),
            pltpu.VMEM((n_lon, kernels * chunk, 3 * width), bf16),
            pltpu.VMEM((3, channels, kernels * width), bf16),
            pltpu.VMEM((channels, width), f32),
            pltpu.VMEM((2, channels, width), bf16),
            pltpu.VMEM((2, channels, width), bf16),
            pltpu.VMEM((2, groups, rows, half), f32),
            pltpu.VMEM((groups, rows, half), f32),
            pltpu.VMEM((n_lat // 2, groups, rows, half), bf16),
            pltpu.VMEM((2, groups, rows, half), f32),
            dma((2, n_lon)), dma((n_lon,)), dma((n_lon,)), dma((n_lon,)), dma((n_lon,)), dma((n_lon,)),
            dma((2, n_lon)), dma((2, n_lon)), dma((2,)), dma((2,)),
            dma((groups,)), dma((groups,)), dma((groups, n_lat // 2)), dma((groups, n_lat // 2 + 1)),
            dma((groups,)), dma((groups,)), dma,
        ],
        compiler_params=pltpu.CompilerParams(
            collective_id=0, has_side_effects=True, vmem_limit_bytes=56 * 1024 * 1024
        ),
        cost_estimate=pl.CostEstimate(
            flops=8_000_000_000, bytes_accessed=3_000_000, transcendentals=0
        ),
    )(
        filter_taps, cycle_counts, cycle_blocks,
        fields.reshape(channels, width), upstream.reshape(channels, width), weights,
    )
    outputs, grad, weight_grad = pl.pallas_call(
        finish,
        out_shape=tuple(jax.ShapeDtypeStruct(held.shape, held.dtype) for held in results),
        in_specs=[vmem] * 3,
        out_specs=[vmem] * 3,
    )(*results)
    return (
        outputs.reshape(fields.shape),
        grad.reshape(fields.shape),
        weight_grad.reshape(kernels, chunk, channels),
    )


def solution(mesh):
    return jax.shard_map(
        body,
        mesh=mesh,
        in_specs=(
            P("groups", "lat", "lon"),
            P("groups", "lat", "lon"),
            P(),
            P("lat", None, None, None, None),
            P("lat"),
            P("lat", None),
        ),
        out_specs=(P("groups", "lat", "lon"), P("groups", "lat", "lon"), P("groups", "lon", None)),
        check_vma=False,
    )
```

```python
import functools

import jax
import jax.numpy as jnp
from jax import lax
from jax.experimental import pallas as pl
from jax.experimental.pallas import tpu as pltpu
from jax.sharding import PartitionSpec as P

HALO = 128
MESH = pl.DeviceIdType.MESH


def finish(*refs):
    count = len(refs) // 2
    for i in range(count):
        refs[count + i][...] = refs[i][...]


def kernel(
    n_lat, n_lon, taps_ref, counts_ref, blocks_ref, f_ref, u_ref, w_hbm, out_ref, grad_ref, wg_ref,
    w_ref, w_turned, f_mine, f_all, u_all, u_chunk, band, resp, met, rg, g_mine, g_out, g_got,
    part, part_got, chip, result,
    zf_s, zf_r, zc_s, zc_r, zu_s, zu_r, lf_s, lf_r, g_s, g_r, p_s, p_r, x_s, x_r, q_s, q_r, w_s,
):
    kernels, channels, _ = w_ref.shape
    width = f_ref.shape[1]
    chunk = u_chunk.shape[1]
    chips = n_lat // 2
    a = lax.axis_index("lat")
    b = lax.axis_index("lon")
    core = lax.rem(a, 2)
    chip_at = a // 2
    twin = a + 1 - 2 * core
    has_up = a < n_lat - 1
    has_down = a > 0

    def lon_peer(step):
        return {"lat": a, "lon": lax.rem(b + step, n_lon)}

    def lat_peer(at):
        return {"lat": at, "lon": b}

    load_w = pltpu.make_async_copy(w_hbm, w_ref, w_s)
    load_w.start()
    barrier = pltpu.get_barrier_semaphore()
    for step in range(1, n_lon):
        pl.semaphore_signal(barrier, inc=1, device_id=lon_peer(step), device_id_type=MESH)
    for step in range(1, n_lat):
        pl.semaphore_signal(
            barrier, inc=1, device_id=lat_peer(lax.rem(a + step, n_lat)), device_id_type=MESH
        )
    f_mine[...] = f_ref[...].T
    pl.semaphore_wait(barrier, n_lon + n_lat - 2)

    def remote(src, dst, send, recv, to):
        return pltpu.make_async_remote_copy(
            src_ref=src, dst_ref=dst, send_sem=send, recv_sem=recv, device_id=to,
            device_id_type=MESH,
        )

    def send_f(step):
        slot = n_lon - step
        return remote(f_mine, f_all.at[slot, 1], zf_s.at[step], zf_r.at[slot], lon_peer(step))

    def send_chunk(step):
        slot = n_lon - step
        start = pl.multiple_of(lax.rem(b + step, n_lon) * chunk, chunk)
        return remote(
            u_ref.at[pl.ds(start, chunk)], u_chunk.at[slot], zc_s.at[step], zc_r.at[slot],
            lon_peer(step),
        )

    def send_u(step):
        slot = n_lon - step
        return remote(u_ref, u_all.at[slot], zu_s.at[step], zu_r.at[slot], lon_peer(step))

    def lat_f(way, slot):
        to = a + 1 if way == 0 else a - 1
        src = f_mine if slot == 0 else f_all.at[slot, 1]
        return remote(
            src, f_all.at[slot, 2 * way], lf_s.at[way, slot], lf_r.at[way, slot], lat_peer(to)
        )

    steps = sorted(range(1, n_lon), key=lambda step: min(step, n_lon - step))
    for step in steps:
        send_chunk(step).start()
    for step in steps:
        send_f(step).start()

    @pl.when(has_up)
    def _():
        lat_f(0, 0).start()

    @pl.when(has_down)
    def _():
        lat_f(1, 0).start()

    slots, block_width = taps_ref.shape[3:]
    lane = lax.broadcasted_iota(jnp.int32, (slots, 4 * HALO), 1)
    which = lax.broadcasted_iota(jnp.int32, (slots, 4 * HALO), 0)
    first = jnp.zeros((slots, 4 * HALO), jnp.int32)
    for s in range(slots):
        first = jnp.where(which == s, HALO + block_width * blocks_ref[0, s], first)
    used = (which < counts_ref[0]) & (lane >= first) & (lane < first + block_width)
    rest = jnp.zeros((slots, 2 * HALO), jnp.float32)
    for k in range(kernels):
        for r in range(3):
            tile = taps_ref[0, k, r].astype(jnp.float32)
            spread = jnp.concatenate([tile] * (2 * HALO // block_width) + [rest], axis=1)
            row = jnp.sum(jnp.where(used, spread, 0.0), axis=0, keepdims=True)
            turned = pltpu.roll(
                jnp.broadcast_to(row, (width, 4 * HALO)), 0, 1, stride=1, stride_axis=0
            ).astype(jnp.bfloat16)
            for d in range(3):
                band[k * width : (k + 1) * width, (3 * d + r) * width : (3 * d + r + 1) * width] = (
                    turned[:, d * width : (d + 1) * width]
                )

    f_all[0, 1] = f_mine[...]

    @pl.when(jnp.logical_not(has_down))
    def _():
        f_all[:, 0] = jnp.zeros((n_lon, width, channels), f_all.dtype)

    @pl.when(jnp.logical_not(has_up))
    def _():
        f_all[:, 2] = jnp.zeros((n_lon, width, channels), f_all.dtype)

    for step in steps:
        slot = n_lon - step
        send_f(step).wait_recv()

        @pl.when(has_up)
        def _():
            lat_f(0, slot).start()

        @pl.when(has_down)
        def _():
            lat_f(1, slot).start()

    for step in (1, n_lon - 1):
        send_u(step).start()

    u_chunk[0] = u_ref[pl.ds(pl.multiple_of(b * chunk, chunk), chunk), :]
    for step in steps:
        send_chunk(step).wait_recv()
    lines = jnp.concatenate(
        [
            jnp.concatenate([u_chunk[(slot + 1 - d) % n_lon] for d in range(3)], axis=1)
            for slot in range(n_lon)
        ],
        axis=0,
    )
    for k in range(kernels):
        rows = slice(k * width, (k + 1) * width)
        taps_k = jnp.concatenate(
            [band[rows, 3 * d * width : 3 * (d + 1) * width] for d in range(3)], axis=0
        )
        spread = jnp.dot(lines, taps_k, preferred_element_type=jnp.float32).astype(jnp.bfloat16)
        for slot in range(n_lon):
            met[slot, k * chunk : (k + 1) * chunk, :] = spread[slot * chunk : (slot + 1) * chunk]

    load_w.wait()
    for k in range(kernels):
        w_turned[k * channels : (k + 1) * channels, :] = w_ref[k].T

    def wait_lat(slot):
        @pl.when(has_down)
        def _():
            lat_f(0, slot).wait_recv()

        @pl.when(has_up)
        def _():
            lat_f(1, slot).wait_recv()

    group = 3 if kernels % 3 == 0 else 1
    groups = kernels // group

    order = [0] + [n_lon - step for step in steps]
    total = jnp.zeros((kernels * chunk, channels), jnp.float32)
    for slot in order[:-1]:
        wait_lat(slot)
        total = total + jnp.dot(
            met[slot], f_all[slot].reshape(3 * width, channels),
            preferred_element_type=jnp.float32,
        )
    for g in range(groups):
        for half in range(2):
            part[half, g] = total[
                g * group * chunk : (g + 1) * group * chunk,
                half * channels // 2 : (half + 1) * channels // 2,
            ]
    wait_lat(order[-1])

    def send_p(g):
        return remote(
            part.at[1 - core, g], part_got.at[g], p_s.at[g], p_r.at[g], lat_peer(twin)
        )

    for g in range(groups):
        piece = jnp.dot(
            met[order[-1], g * group * chunk : (g + 1) * group * chunk, :],
            f_all[order[-1]].reshape(3 * width, channels),
            preferred_element_type=jnp.float32,
        )
        for half in range(2):
            part[half, g] += piece[:, half * channels // 2 : (half + 1) * channels // 2]
        send_p(g).start()

    window = jnp.concatenate(
        [f_all[slot].reshape(3 * width, channels) for slot in (n_lon - 1, 0, 1)], axis=0
    )

    def convolve(g):
        got = jnp.dot(
            band[g * group * width : (g + 1) * group * width, :], window,
            preferred_element_type=jnp.float32,
        ).astype(jnp.bfloat16)
        for k in range(group):
            resp[:, (g * group + k) * channels : (g * group + k + 1) * channels] = got[
                k * width : (k + 1) * width
            ]

    def send_x(g, step):
        to = lax.rem(a + 2 * step, n_lat)
        return remote(
            chip.at[chip_at, g], chip.at[chip_at, g], x_s.at[g, step],
            x_r.at[g, chips - step], lat_peer(to),
        )

    def got_x(g, step):
        at = lax.rem(chip_at + chips - step, chips)
        return remote(
            chip.at[at, g], chip.at[at, g], x_s.at[g, step], x_r.at[g, chips - step],
            lat_peer(twin),
        )

    for g in range(groups):
        convolve(g)
        send_p(g).wait_recv()
        chip[chip_at, g] = (part[core, g] + part_got[g]).astype(chip.dtype)
        for step in range(1, chips):
            send_x(g, step).start()

    u_all[0] = u_ref[...]
    for step in (1, n_lon - 1):
        send_u(step).wait_recv()
    u_wide = jnp.concatenate([u_all[n_lon - 1], u_all[0], u_all[1]], axis=1)
    for k in range(kernels):
        mixed = jnp.dot(
            w_turned[k * channels : (k + 1) * channels, :], u_wide,
            preferred_element_type=jnp.float32,
        ).astype(jnp.bfloat16)
        for j in range(3):
            rg[j, :, k * width : (k + 1) * width] = mixed[:, j * width : (j + 1) * width]
    terms = jnp.zeros((channels, 3 * width), jnp.float32)
    for j in range(3):
        terms = terms + jnp.dot(
            rg[j], band[:, (2 - j) * 3 * width : (3 - j) * 3 * width],
            preferred_element_type=jnp.float32,
        )
    g_mine[...] = terms[:, width : 2 * width]
    g_out[0] = terms[:, 2 * width :].astype(g_out.dtype)
    g_out[1] = terms[:, :width].astype(g_out.dtype)

    def send_g(way):
        to = a + 1 if way == 0 else a - 1
        return remote(g_out.at[way], g_got.at[way], g_s.at[way], g_r.at[way], lat_peer(to))

    @pl.when(has_up)
    def _():
        send_g(0).start()

    @pl.when(has_down)
    def _():
        send_g(1).start()

    mixed = jnp.dot(resp[...], w_turned[...], preferred_element_type=jnp.float32)
    out_ref[...] = mixed.astype(out_ref.dtype).T

    def send_q(g):
        return remote(result.at[core, g], result.at[core, g], q_s.at[g], q_r.at[g], lat_peer(twin))

    def got_q(g):
        return remote(
            result.at[1 - core, g], result.at[1 - core, g], q_s.at[g], q_r.at[g], lat_peer(twin)
        )

    for g in range(groups):
        for step in range(1, chips):
            got_x(g, step).wait_recv()
        total = chip[0, g].astype(jnp.float32)
        for at in range(1, chips):
            total = total + chip[at, g].astype(jnp.float32)
        result[core, g] = total
        send_q(g).start()

    @pl.when(has_down)
    def _():
        send_g(0).wait_recv()

    @pl.when(has_up)
    def _():
        send_g(1).wait_recv()

    below = jnp.where(has_down, g_got[0].astype(jnp.float32), 0.0)
    above = jnp.where(has_up, g_got[1].astype(jnp.float32), 0.0)
    grad_ref[...] = (g_mine[...] + below + above).astype(grad_ref.dtype)

    for g in range(groups):
        got_q(g).wait_recv()
        rows = slice(g * group * chunk, (g + 1) * group * chunk)
        wg_ref[rows, : channels // 2] = result[0, g]
        wg_ref[rows, channels // 2 :] = result[1, g]

    for step in range(1, n_lon):
        send_f(step).wait_send()
        send_chunk(step).wait_send()
    for step in (1, n_lon - 1):
        send_u(step).wait_send()
    for slot in range(n_lon):
        @pl.when(has_up)
        def _():
            lat_f(0, slot).wait_send()

        @pl.when(has_down)
        def _():
            lat_f(1, slot).wait_send()

    @pl.when(has_up)
    def _():
        send_g(0).wait_send()

    @pl.when(has_down)
    def _():
        send_g(1).wait_send()

    for g in range(groups):
        send_p(g).wait_send()
        for step in range(1, chips):
            send_x(g, step).wait_send()
        send_q(g).wait_send()


def body(fields, upstream, weights, filter_taps, cycle_counts, cycle_blocks):
    channels, _, width = fields.shape
    kernels = weights.shape[0]
    n_lat, n_lon = lax.axis_size("lat"), lax.axis_size("lon")
    chunk = channels // n_lon
    groups = kernels // 3 if kernels % 3 == 0 else kernels
    rows, half = kernels // groups * chunk, channels // 2
    bf16, f32 = jnp.bfloat16, jnp.float32
    dma = pltpu.SemaphoreType.DMA
    vmem = pl.BlockSpec(memory_space=pltpu.VMEM)
    smem = pl.BlockSpec(memory_space=pltpu.SMEM)
    anywhere = pl.BlockSpec(memory_space=pl.ANY)
    results = pl.pallas_call(
        functools.partial(kernel, n_lat, n_lon),
        out_shape=(
            jax.ShapeDtypeStruct((channels, width), bf16),
            jax.ShapeDtypeStruct((channels, width), bf16),
            jax.ShapeDtypeStruct((kernels * chunk, channels), f32),
        ),
        in_specs=[vmem, smem, smem, vmem, vmem, anywhere],
        out_specs=[vmem] * 3,
        scratch_shapes=[
            pltpu.VMEM(weights.shape, bf16),
            pltpu.VMEM((kernels * channels, channels), bf16),
            pltpu.VMEM((width, channels), bf16),
            pltpu.VMEM((n_lon, 3, width, channels), bf16),
            pltpu.VMEM((n_lon, channels, width), bf16),
            pltpu.VMEM((n_lon, chunk, width), bf16),
            pltpu.VMEM((kernels * width, 9 * width), bf16),
            pltpu.VMEM((width, kernels * channels), bf16),
            pltpu.VMEM((n_lon, kernels * chunk, 3 * width), bf16),
            pltpu.VMEM((3, channels, kernels * width), bf16),
            pltpu.VMEM((channels, width), f32),
            pltpu.VMEM((2, channels, width), bf16),
            pltpu.VMEM((2, channels, width), bf16),
            pltpu.VMEM((2, groups, rows, half), f32),
            pltpu.VMEM((groups, rows, half), f32),
            pltpu.VMEM((n_lat // 2, groups, rows, half), bf16),
            pltpu.VMEM((2, groups, rows, half), f32),
            dma((n_lon,)), dma((n_lon,)), dma((n_lon,)), dma((n_lon,)), dma((n_lon,)), dma((n_lon,)),
            dma((2, n_lon)), dma((2, n_lon)), dma((2,)), dma((2,)),
            dma((groups,)), dma((groups,)), dma((groups, n_lat // 2)), dma((groups, n_lat // 2 + 1)),
            dma((groups,)), dma((groups,)), dma,
        ],
        compiler_params=pltpu.CompilerParams(
            collective_id=0, has_side_effects=True, vmem_limit_bytes=56 * 1024 * 1024
        ),
        cost_estimate=pl.CostEstimate(
            flops=8_000_000_000, bytes_accessed=3_000_000, transcendentals=0
        ),
    )(
        filter_taps, cycle_counts, cycle_blocks,
        fields.reshape(channels, width), upstream.reshape(channels, width), weights,
    )
    outputs, grad, weight_grad = pl.pallas_call(
        finish,
        out_shape=tuple(jax.ShapeDtypeStruct(held.shape, held.dtype) for held in results),
        in_specs=[vmem] * 3,
        out_specs=[vmem] * 3,
    )(*results)
    return (
        outputs.reshape(fields.shape),
        grad.reshape(fields.shape),
        weight_grad.reshape(kernels, chunk, channels),
    )


def solution(mesh):
    return jax.shard_map(
        body,
        mesh=mesh,
        in_specs=(
            P("groups", "lat", "lon"),
            P("groups", "lat", "lon"),
            P(),
            P("lat", None, None, None, None),
            P("lat"),
            P("lat", None),
        ),
        out_specs=(P("groups", "lat", "lon"), P("groups", "lat", "lon"), P("groups", "lon", None)),
        check_vma=False,
    )
```

```python
import functools

import jax
import jax.numpy as jnp
from jax import lax
from jax.experimental import pallas as pl
from jax.experimental.pallas import tpu as pltpu
from jax.sharding import PartitionSpec as P

HALO = 128
MESH = pl.DeviceIdType.MESH


def finish(*refs):
    count = len(refs) // 2
    for i in range(count):
        refs[count + i][...] = refs[i][...]


def kernel(
    n_lat, n_lon, taps_ref, counts_ref, blocks_ref, f_ref, u_ref, w_hbm, out_ref, grad_ref, wg_ref,
    w_ref, w_turned, f_mine, f_all, u_all, u_chunk, band, resp, met, rg, g_mine, g_out, g_got,
    part, part_got, chip, result,
    zf_s, zf_r, zc_s, zc_r, zu_s, zu_r, lf_s, lf_r, g_s, g_r, p_s, p_r, x_s, x_r, q_s, q_r, w_s,
):
    kernels, channels, _ = w_ref.shape
    width = f_ref.shape[1]
    chunk = u_chunk.shape[1]
    chips = n_lat // 2
    a = lax.axis_index("lat")
    b = lax.axis_index("lon")
    core = lax.rem(a, 2)
    chip_at = a // 2
    twin = a + 1 - 2 * core
    has_up = a < n_lat - 1
    has_down = a > 0

    def lon_peer(step):
        return {"lat": a, "lon": lax.rem(b + step, n_lon)}

    def lat_peer(at):
        return {"lat": at, "lon": b}

    load_w = pltpu.make_async_copy(w_hbm, w_ref, w_s)
    load_w.start()
    barrier = pltpu.get_barrier_semaphore()
    for step in range(1, n_lon):
        pl.semaphore_signal(barrier, inc=1, device_id=lon_peer(step), device_id_type=MESH)
    for step in range(1, n_lat):
        pl.semaphore_signal(
            barrier, inc=1, device_id=lat_peer(lax.rem(a + step, n_lat)), device_id_type=MESH
        )
    f_mine[...] = f_ref[...].T
    pl.semaphore_wait(barrier, n_lon + n_lat - 2)

    def remote(src, dst, send, recv, to):
        return pltpu.make_async_remote_copy(
            src_ref=src, dst_ref=dst, send_sem=send, recv_sem=recv, device_id=to,
            device_id_type=MESH,
        )

    def send_f(step):
        slot = n_lon - step
        return remote(f_mine, f_all.at[slot, 1], zf_s.at[step], zf_r.at[slot], lon_peer(step))

    def send_chunk(step):
        slot = n_lon - step
        start = pl.multiple_of(lax.rem(b + step, n_lon) * chunk, chunk)
        return remote(
            u_ref.at[pl.ds(start, chunk)], u_chunk.at[slot], zc_s.at[step], zc_r.at[slot],
            lon_peer(step),
        )

    def send_u(step):
        slot = n_lon - step
        return remote(u_ref, u_all.at[slot], zu_s.at[step], zu_r.at[slot], lon_peer(step))

    def lat_f(way, slot):
        to = a + 1 if way == 0 else a - 1
        src = f_mine if slot == 0 else f_all.at[slot, 1]
        return remote(
            src, f_all.at[slot, 2 * way], lf_s.at[way, slot], lf_r.at[way, slot], lat_peer(to)
        )

    steps = sorted(range(1, n_lon), key=lambda step: min(step, n_lon - step))
    for step in steps:
        send_chunk(step).start()
    for step in steps:
        send_f(step).start()

    @pl.when(has_up)
    def _():
        lat_f(0, 0).start()

    @pl.when(has_down)
    def _():
        lat_f(1, 0).start()

    def pass_on(step):
        slot = n_lon - step
        send_f(step).wait_recv()

        @pl.when(has_up)
        def _():
            lat_f(0, slot).start()

        @pl.when(has_down)
        def _():
            lat_f(1, slot).start()

    slots, block_width = taps_ref.shape[3:]
    lane = lax.broadcasted_iota(jnp.int32, (slots, 4 * HALO), 1)
    which = lax.broadcasted_iota(jnp.int32, (slots, 4 * HALO), 0)
    first = jnp.zeros((slots, 4 * HALO), jnp.int32)
    for s in range(slots):
        first = jnp.where(which == s, HALO + block_width * blocks_ref[0, s], first)
    used = (which < counts_ref[0]) & (lane >= first) & (lane < first + block_width)
    rest = jnp.zeros((slots, 2 * HALO), jnp.float32)
    for k in range(kernels):
        if k == 2 * kernels // 3:
            for step in steps[:2]:
                pass_on(step)
        for r in range(3):
            tile = taps_ref[0, k, r].astype(jnp.float32)
            spread = jnp.concatenate([tile] * (2 * HALO // block_width) + [rest], axis=1)
            row = jnp.sum(jnp.where(used, spread, 0.0), axis=0, keepdims=True)
            turned = pltpu.roll(
                jnp.broadcast_to(row, (width, 4 * HALO)), 0, 1, stride=1, stride_axis=0
            ).astype(jnp.bfloat16)
            for d in range(3):
                band[k * width : (k + 1) * width, (3 * d + r) * width : (3 * d + r + 1) * width] = (
                    turned[:, d * width : (d + 1) * width]
                )

    f_all[0, 1] = f_mine[...]

    @pl.when(jnp.logical_not(has_down))
    def _():
        f_all[:, 0] = jnp.zeros((n_lon, width, channels), f_all.dtype)

    @pl.when(jnp.logical_not(has_up))
    def _():
        f_all[:, 2] = jnp.zeros((n_lon, width, channels), f_all.dtype)

    for step in steps[2:]:
        pass_on(step)

    for step in (1, n_lon - 1):
        send_u(step).start()

    u_chunk[0] = u_ref[pl.ds(pl.multiple_of(b * chunk, chunk), chunk), :]
    for step in steps:
        send_chunk(step).wait_recv()
    lines = jnp.concatenate(
        [
            jnp.concatenate([u_chunk[(slot + 1 - d) % n_lon] for d in range(3)], axis=1)
            for slot in range(n_lon)
        ],
        axis=0,
    )
    for k in range(kernels):
        rows = slice(k * width, (k + 1) * width)
        taps_k = jnp.concatenate(
            [band[rows, 3 * d * width : 3 * (d + 1) * width] for d in range(3)], axis=0
        )
        spread = jnp.dot(lines, taps_k, preferred_element_type=jnp.float32).astype(jnp.bfloat16)
        for slot in range(n_lon):
            met[slot, k * chunk : (k + 1) * chunk, :] = spread[slot * chunk : (slot + 1) * chunk]

    load_w.wait()
    for k in range(kernels):
        w_turned[k * channels : (k + 1) * channels, :] = w_ref[k].T

    def wait_lat(slot):
        @pl.when(has_down)
        def _():
            lat_f(0, slot).wait_recv()

        @pl.when(has_up)
        def _():
            lat_f(1, slot).wait_recv()

    group = 3 if kernels % 3 == 0 else 1
    groups = kernels // group

    order = [0] + [n_lon - step for step in steps]
    total = jnp.zeros((kernels * chunk, channels), jnp.float32)
    for slot in order[:-1]:
        wait_lat(slot)
        total = total + jnp.dot(
            met[slot], f_all[slot].reshape(3 * width, channels),
            preferred_element_type=jnp.float32,
        )
    for g in range(groups):
        for half in range(2):
            part[half, g] = total[
                g * group * chunk : (g + 1) * group * chunk,
                half * channels // 2 : (half + 1) * channels // 2,
            ]
    wait_lat(order[-1])

    def send_p(g):
        return remote(
            part.at[1 - core, g], part_got.at[g], p_s.at[g], p_r.at[g], lat_peer(twin)
        )

    for g in range(groups):
        piece = jnp.dot(
            met[order[-1], g * group * chunk : (g + 1) * group * chunk, :],
            f_all[order[-1]].reshape(3 * width, channels),
            preferred_element_type=jnp.float32,
        )
        for half in range(2):
            part[half, g] += piece[:, half * channels // 2 : (half + 1) * channels // 2]
        send_p(g).start()

    window = jnp.concatenate(
        [f_all[slot].reshape(3 * width, channels) for slot in (n_lon - 1, 0, 1)], axis=0
    )

    def convolve(g):
        got = jnp.dot(
            band[g * group * width : (g + 1) * group * width, :], window,
            preferred_element_type=jnp.float32,
        ).astype(jnp.bfloat16)
        for k in range(group):
            resp[:, (g * group + k) * channels : (g * group + k + 1) * channels] = got[
                k * width : (k + 1) * width
            ]

    def send_x(g, step):
        to = lax.rem(a + 2 * step, n_lat)
        return remote(
            chip.at[chip_at, g], chip.at[chip_at, g], x_s.at[g, step],
            x_r.at[g, chips - step], lat_peer(to),
        )

    def got_x(g, step):
        at = lax.rem(chip_at + chips - step, chips)
        return remote(
            chip.at[at, g], chip.at[at, g], x_s.at[g, step], x_r.at[g, chips - step],
            lat_peer(twin),
        )

    for g in range(groups):
        convolve(g)
        send_p(g).wait_recv()
        chip[chip_at, g] = (part[core, g] + part_got[g]).astype(chip.dtype)
        for step in range(1, chips):
            send_x(g, step).start()

    u_all[0] = u_ref[...]
    for step in (1, n_lon - 1):
        send_u(step).wait_recv()
    u_wide = jnp.concatenate([u_all[n_lon - 1], u_all[0], u_all[1]], axis=1)
    for k in range(kernels):
        mixed = jnp.dot(
            w_turned[k * channels : (k + 1) * channels, :], u_wide,
            preferred_element_type=jnp.float32,
        ).astype(jnp.bfloat16)
        for j in range(3):
            rg[j, :, k * width : (k + 1) * width] = mixed[:, j * width : (j + 1) * width]
    terms = jnp.zeros((channels, 3 * width), jnp.float32)
    for j in range(3):
        terms = terms + jnp.dot(
            rg[j], band[:, (2 - j) * 3 * width : (3 - j) * 3 * width],
            preferred_element_type=jnp.float32,
        )
    g_mine[...] = terms[:, width : 2 * width]
    g_out[0] = terms[:, 2 * width :].astype(g_out.dtype)
    g_out[1] = terms[:, :width].astype(g_out.dtype)

    def send_g(way):
        to = a + 1 if way == 0 else a - 1
        return remote(g_out.at[way], g_got.at[way], g_s.at[way], g_r.at[way], lat_peer(to))

    @pl.when(has_up)
    def _():
        send_g(0).start()

    @pl.when(has_down)
    def _():
        send_g(1).start()

    mixed = jnp.dot(resp[...], w_turned[...], preferred_element_type=jnp.float32)
    out_ref[...] = mixed.astype(out_ref.dtype).T

    def send_q(g):
        return remote(result.at[core, g], result.at[core, g], q_s.at[g], q_r.at[g], lat_peer(twin))

    def got_q(g):
        return remote(
            result.at[1 - core, g], result.at[1 - core, g], q_s.at[g], q_r.at[g], lat_peer(twin)
        )

    for g in range(groups):
        for step in range(1, chips):
            got_x(g, step).wait_recv()
        total = chip[0, g].astype(jnp.float32)
        for at in range(1, chips):
            total = total + chip[at, g].astype(jnp.float32)
        result[core, g] = total
        send_q(g).start()

    @pl.when(has_down)
    def _():
        send_g(0).wait_recv()

    @pl.when(has_up)
    def _():
        send_g(1).wait_recv()

    below = jnp.where(has_down, g_got[0].astype(jnp.float32), 0.0)
    above = jnp.where(has_up, g_got[1].astype(jnp.float32), 0.0)
    grad_ref[...] = (g_mine[...] + below + above).astype(grad_ref.dtype)

    for g in range(groups):
        got_q(g).wait_recv()
        rows = slice(g * group * chunk, (g + 1) * group * chunk)
        wg_ref[rows, : channels // 2] = result[0, g]
        wg_ref[rows, channels // 2 :] = result[1, g]

    for step in range(1, n_lon):
        send_f(step).wait_send()
        send_chunk(step).wait_send()
    for step in (1, n_lon - 1):
        send_u(step).wait_send()
    for slot in range(n_lon):
        @pl.when(has_up)
        def _():
            lat_f(0, slot).wait_send()

        @pl.when(has_down)
        def _():
            lat_f(1, slot).wait_send()

    @pl.when(has_up)
    def _():
        send_g(0).wait_send()

    @pl.when(has_down)
    def _():
        send_g(1).wait_send()

    for g in range(groups):
        send_p(g).wait_send()
        for step in range(1, chips):
            send_x(g, step).wait_send()
        send_q(g).wait_send()


def body(fields, upstream, weights, filter_taps, cycle_counts, cycle_blocks):
    channels, _, width = fields.shape
    kernels = weights.shape[0]
    n_lat, n_lon = lax.axis_size("lat"), lax.axis_size("lon")
    chunk = channels // n_lon
    groups = kernels // 3 if kernels % 3 == 0 else kernels
    rows, half = kernels // groups * chunk, channels // 2
    bf16, f32 = jnp.bfloat16, jnp.float32
    dma = pltpu.SemaphoreType.DMA
    vmem = pl.BlockSpec(memory_space=pltpu.VMEM)
    smem = pl.BlockSpec(memory_space=pltpu.SMEM)
    anywhere = pl.BlockSpec(memory_space=pl.ANY)
    results = pl.pallas_call(
        functools.partial(kernel, n_lat, n_lon),
        out_shape=(
            jax.ShapeDtypeStruct((channels, width), bf16),
            jax.ShapeDtypeStruct((channels, width), bf16),
            jax.ShapeDtypeStruct((kernels * chunk, channels), f32),
        ),
        in_specs=[vmem, smem, smem, vmem, vmem, anywhere],
        out_specs=[vmem] * 3,
        scratch_shapes=[
            pltpu.VMEM(weights.shape, bf16),
            pltpu.VMEM((kernels * channels, channels), bf16),
            pltpu.VMEM((width, channels), bf16),
            pltpu.VMEM((n_lon, 3, width, channels), bf16),
            pltpu.VMEM((n_lon, channels, width), bf16),
            pltpu.VMEM((n_lon, chunk, width), bf16),
            pltpu.VMEM((kernels * width, 9 * width), bf16),
            pltpu.VMEM((width, kernels * channels), bf16),
            pltpu.VMEM((n_lon, kernels * chunk, 3 * width), bf16),
            pltpu.VMEM((3, channels, kernels * width), bf16),
            pltpu.VMEM((channels, width), f32),
            pltpu.VMEM((2, channels, width), bf16),
            pltpu.VMEM((2, channels, width), bf16),
            pltpu.VMEM((2, groups, rows, half), f32),
            pltpu.VMEM((groups, rows, half), f32),
            pltpu.VMEM((n_lat // 2, groups, rows, half), bf16),
            pltpu.VMEM((2, groups, rows, half), f32),
            dma((n_lon,)), dma((n_lon,)), dma((n_lon,)), dma((n_lon,)), dma((n_lon,)), dma((n_lon,)),
            dma((2, n_lon)), dma((2, n_lon)), dma((2,)), dma((2,)),
            dma((groups,)), dma((groups,)), dma((groups, n_lat // 2)), dma((groups, n_lat // 2 + 1)),
            dma((groups,)), dma((groups,)), dma,
        ],
        compiler_params=pltpu.CompilerParams(
            collective_id=0, has_side_effects=True, vmem_limit_bytes=56 * 1024 * 1024
        ),
        cost_estimate=pl.CostEstimate(
            flops=8_000_000_000, bytes_accessed=3_000_000, transcendentals=0
        ),
    )(
        filter_taps, cycle_counts, cycle_blocks,
        fields.reshape(channels, width), upstream.reshape(channels, width), weights,
    )
    outputs, grad, weight_grad = pl.pallas_call(
        finish,
        out_shape=tuple(jax.ShapeDtypeStruct(held.shape, held.dtype) for held in results),
        in_specs=[vmem] * 3,
        out_specs=[vmem] * 3,
    )(*results)
    return (
        outputs.reshape(fields.shape),
        grad.reshape(fields.shape),
        weight_grad.reshape(kernels, chunk, channels),
    )


def solution(mesh):
    return jax.shard_map(
        body,
        mesh=mesh,
        in_specs=(
            P("groups", "lat", "lon"),
            P("groups", "lat", "lon"),
            P(),
            P("lat", None, None, None, None),
            P("lat"),
            P("lat", None),
        ),
        out_specs=(P("groups", "lat", "lon"), P("groups", "lat", "lon"), P("groups", "lon", None)),
        check_vma=False,
    )
```
